128 devices in a mesh: group: 4 (over z), dom: 32 (over y, x, core).
Axes of the slice: x: 4, y: 4, z: 4, core: 2. Of those that a mesh axis runs over, the one named last changes fastest.
Arguments:
- feats: bfloat16 [262144, 256], P(('group', 'dom')), may hold values from -6 to 6
- edge_src: int32 [128, 8192], P(('group', 'dom')), may hold values from 0 to 2047, as said below
- edge_slot: int32 [128, 8192], P(('group', 'dom')), may hold values from 0 to 1535
- slot_counts: int32 [128, 32], P(('group', 'dom')), may hold values from 36 to 48, as said below
- replica_row: int32 [128, 32, 48], P(('group', 'dom')), may hold values from 0 to 2047
- stale_agg: bfloat16 [262144, 256], P(('group', 'dom')), may hold values from -6 to 6
- bin_ages: int32 [2048], P(('group', 'dom')), may hold values from 0 to 7
- cotangent: bfloat16 [262144, 256], P(('group', 'dom')), may hold values from -6 to 6
- w_self: bfloat16 [256, 256], replicated, may hold values from -0.375 to 0.375
- w_neigh: bfloat16 [256, 256], replicated, may hold values from -0.375 to 0.375
Outputs:
- hidden: bfloat16 [262144, 256], P(('group', 'dom'))
- feat_grad: bfloat16 [262144, 256], P(('group', 'dom'))
- new_self: float32 [256, 256], replicated
- new_neigh: float32 [256, 256], replicated
The draws below stay inside these ranges and needn't reach their ends.
Inputs may be any that keep to these rules, and one draw needn't show every extreme that they name: `slot_counts`: in every row some entry equals 48. `edge_src`: edges come in tiles of 128; the sources of tile t lie in rows 128 * (t mod (16)) to 128 * (t mod (16)) + 127.
All inputs are finite; a program needn't handle non-finite values.
Results may differ from the reference program's by a relative error of at most 0.0056.
Values may be sent and summed in bfloat16 or wider, within the bound.
No kernel may reach another device: no remote copies, remote signals or barrier semaphores. Data moves between devices by JAX's collectives and lax.ppermute only.
A program may use at most 64 MiB of HBM per device.

```python
import jax
import jax.numpy as jnp
from jax import lax

D = 256
H = 256
V_DEV = 2048
E_DEV = 8192
CAP = 48
VERTS = 262144
SLOTS = 1536
PARTITION_TOTAL = 128
BINS = 2048
N_GROUP = 4
N_DOM = 32


def draw_slot_counts(key, part):
    key = jax.random.fold_in(key, 11)
    first_key, second_key = jax.random.split(key)
    counts = jax.random.randint(first_key, (N_GROUP * N_DOM, N_DOM), 3 * CAP // 4, CAP + 1)
    picked = jax.random.randint(second_key, (N_GROUP * N_DOM,), 0, N_DOM)
    column = jnp.arange(N_DOM)[None, :]
    return jnp.where(column == picked[:, None], CAP, counts).astype(jnp.int32)


def draw_edge_src(key, part):
    key = jax.random.fold_in(key, 23)
    inside_partition = jax.random.randint(key, (N_GROUP * N_DOM, E_DEV), 0, 128)
    tiles = jnp.arange(E_DEV, dtype=jnp.int32) // 128
    base = tiles % (V_DEV // 128) * 128
    return (base[None, :] + inside_partition).astype(jnp.int32)


def with_ends(entries, stream_key, least, largest):
    longest = entries.shape.index(max(entries.shape))
    spots = []
    for shift in (0, 1):
        where = [jax.random.randint(jax.random.fold_in(stream_key, axis), (), 0, length) for axis, length in enumerate(entries.shape)]
        where[longest] = (where[longest] + shift) % entries.shape[longest]
        spots.append(tuple(where))
    return entries.at[spots[0]].set(least).at[spots[1]].set(largest)


def shard_levels(own_key, extent, cuts, smallest, high):
    level, own = 1.0, jax.random.fold_in(own_key, 6)
    for dim, parts in cuts:
        heights = jnp.exp(jax.random.uniform(jax.random.fold_in(own, dim), (parts,), jnp.float32, smallest / len(cuts), high / len(cuts)))
        level = level * jnp.repeat(heights, extent[dim] // parts).reshape([-1 if axis == dim else 1 for axis in range(len(extent))])
    return level


def gaussian(key, dims, deviation, most, cuts=(), kind=jnp.bfloat16):
    array = jax.random.normal(key, dims, jnp.float32) * deviation
    if len(cuts) > 0:
        array = shard_levels(key, dims, cuts, -0.22, 0.18) * array
    return jnp.clip(array, min=-most, max=most).astype(kind)


def setup_inputs(seed: int = 0) -> dict:
    keys = jax.random.split(jax.random.key(seed), 11)
    return {
        "feats": gaussian(keys[0], (VERTS, D), 1.0, 6.0, ((0, 128),)),
        "edge_src": draw_edge_src(jax.random.fold_in(keys[10], 71), 0),
        "edge_slot": with_ends(jax.random.randint(keys[2], (PARTITION_TOTAL, E_DEV), 0, SLOTS), jax.random.fold_in(keys[2], 1), 0, SLOTS - 1).astype(jnp.int32),
        "slot_counts": draw_slot_counts(jax.random.fold_in(keys[10], 71), 0),
        "replica_row": with_ends(jax.random.randint(keys[4], (PARTITION_TOTAL, N_DOM, CAP), 0, V_DEV), jax.random.fold_in(keys[4], 1), 0, V_DEV - 1).astype(jnp.int32),
        "stale_agg": gaussian(keys[5], (VERTS, D), 1.0, 6.0, ((0, 128),)),
        "bin_ages": with_ends(jax.random.randint(keys[6], (BINS,), 0, 8), jax.random.fold_in(keys[6], 1), 0, 7).astype(jnp.int32),
        "cotangent": gaussian(keys[7], (VERTS, H), 1.0, 6.0, ((0, 128),)),
        "w_self": gaussian(keys[8], (D, H), D ** -0.5, 0.375),
        "w_neigh": gaussian(keys[9], (D, H), D ** -0.5, 0.375),
    }


def edge_sum(packed):
    rows_feat, sources, targets = packed
    return jax.ops.segment_sum(rows_feat[sources].astype(jnp.float32), targets, num_segments=N_DOM * CAP)

def edge_back(packed):
    slot_vals, targets, sources = packed
    return jax.ops.segment_sum(slot_vals[targets].astype(jnp.float32), sources, num_segments=V_DEV)

def reference(feats, edge_src, edge_slot, slot_counts, replica_row, stale_agg, bin_ages, cotangent, w_self, w_neigh):
    ndev = N_GROUP * N_DOM
    width = feats.shape[1]
    blocks = feats.reshape(ndev, V_DEV, width)
    slot_live = jnp.arange(CAP)[None, None, :] < slot_counts[:, :, None]
    partial_value_rows = lax.map(edge_sum, (blocks, edge_src, edge_slot)).reshape(ndev, N_DOM, CAP, width)
    partial_value_rows = jnp.where(slot_live[..., None], partial_value_rows, jnp.float32(0.0)).astype(jnp.bfloat16)
    devices = jnp.arange(ndev, dtype=jnp.int32)
    target = (devices // N_DOM)[:, None] * N_DOM + jnp.arange(N_DOM, dtype=jnp.int32)[None, :]
    vertex_ids = (target[:, :, None] * V_DEV + replica_row).reshape(-1).astype(jnp.int32)
    summed = jax.ops.segment_sum(partial_value_rows.reshape(-1, width).astype(jnp.float32), vertex_ids, num_segments=VERTS)
    age_factor = jnp.repeat(1.0 / (1.0 + bin_ages.astype(jnp.float32)), 128)
    aggregate = summed + stale_agg.astype(jnp.float32) * age_factor[:, None]
    inverse = lax.rsqrt(lax.optimization_barrier(jnp.mean(aggregate * aggregate, axis=1, keepdims=True)) + 1e-05)
    normed = (aggregate * inverse).astype(jnp.bfloat16)
    preact = jnp.dot(feats, w_self, preferred_element_type=jnp.float32) + jnp.dot(normed, w_neigh, preferred_element_type=jnp.float32)
    sigmoid_pre = jax.nn.sigmoid(preact)
    hidden = (preact * sigmoid_pre).astype(jnp.bfloat16)
    grad_pre = (cotangent.astype(jnp.float32) * sigmoid_pre * (1.0 + preact * (1.0 - sigmoid_pre))).astype(jnp.bfloat16)
    grad_self = jnp.dot(feats.T, grad_pre, preferred_element_type=jnp.float32)
    grad_neigh = jnp.dot(normed.T, grad_pre, preferred_element_type=jnp.float32)
    grad_normed = jnp.dot(grad_pre, w_neigh.T, preferred_element_type=jnp.float32)
    inner = lax.optimization_barrier(jnp.mean(grad_normed * aggregate, axis=1, keepdims=True))
    grad_agg = (inverse * (grad_normed - aggregate * inverse * inverse * inner)).astype(jnp.bfloat16)
    slot_grads = jnp.where(slot_live[..., None], grad_agg[vertex_ids].reshape(ndev, N_DOM, CAP, width), jnp.zeros((), jnp.bfloat16))
    slot_grads = slot_grads.reshape(ndev, N_DOM * CAP, width)
    edge_grads = lax.map(edge_back, (slot_grads, edge_slot, edge_src)).reshape(VERTS, width)
    feat_grad = (jnp.dot(grad_pre, w_self.T, preferred_element_type=jnp.float32) + edge_grads).astype(jnp.bfloat16)
    grad_norm = jnp.sqrt(jnp.sum(grad_self * grad_self) + jnp.sum(grad_neigh * grad_neigh))
    clip_scale = jnp.minimum(1.0, 1.0 / grad_norm)
    new_self = w_self.astype(jnp.float32) - 8.0 * clip_scale * grad_self
    new_neigh = w_neigh.astype(jnp.float32) - 8.0 * clip_scale * grad_neigh
    return (hidden, feat_grad, new_self, new_neigh)
```

```python
import functools

import jax
import jax.numpy as jnp
from jax import lax
from jax.experimental import pallas as pl
from jax.experimental.pallas import tpu as pltpu
from jax.sharding import PartitionSpec as P

BF = jnp.bfloat16
F32 = jnp.float32
TILE = 128
ROWS = 512
INDEX_ROWS = 16
NN = (((1,), (0,)), ((), ()))
NT = (((1,), (1,)), ((), ()))
TN = (((0,), (0,)), ((), ()))
VMEM_BYTES = 48 * 1024 * 1024


def dot(a, b, dims):
    return lax.dot_general(a, b, dims, preferred_element_type=F32)


def mask(cond):
    return jnp.where(cond, 1.0, 0.0).astype(BF)


def bin_edges(ref, b, bins, repeats):
    return jnp.concatenate(
        [ref[:, pl.ds(pl.multiple_of((g * bins + b) * TILE, TILE), TILE)] for g in range(repeats)],
        axis=1,
    )


def bin_indicators(src_ref, slot_ref, b, bins, repeats, slots):
    src = bin_edges(src_ref, b, bins, repeats) & (TILE - 1)
    slot = bin_edges(slot_ref, b, bins, repeats)
    row = lax.broadcasted_iota(jnp.int32, (TILE, src.shape[1]), 0)
    source = mask(row == src)
    low = mask(row == (slot & (TILE - 1)))
    high = slot >> 7
    blocks = [low * mask(high == h) for h in range(slots // TILE)]
    return source, blocks


def scatter_kernel(counts_ref, rows_ref, src_ref, slot_ref, feats_ref, out_ref, adj_ref):
    slots, verts = adj_ref.shape
    peers, cap = rows_ref.shape
    bins = verts // TILE
    repeats = src_ref.shape[1] // verts

    def one_bin(b, carry):
        source, blocks = bin_indicators(src_ref, slot_ref, b, bins, repeats, slots)
        column = pl.ds(pl.multiple_of(b * TILE, TILE), TILE)
        for h, block in enumerate(blocks):
            adj_ref[h * TILE : (h + 1) * TILE, column] = dot(block, source, NT).astype(BF)
        return carry

    lax.fori_loop(0, bins, one_bin, 0)
    sub = lax.broadcasted_iota(jnp.int32, (INDEX_ROWS, cap), 0)
    slot_in_peer = lax.broadcasted_iota(jnp.int32, (cap, 2 * TILE), 0)
    step = 8
    for first in range(0, peers, step):
        rows = dot(adj_ref[first * cap : (first + step) * cap, :], feats_ref[...], NN)
        for q in range(first, first + step):
            part = rows[(q - first) * cap : (q - first + 1) * cap, :]
            part = jnp.where(slot_in_peer < counts_ref[0, q], part, 0.0).astype(BF)
            out_ref[q, 0:cap, :] = part[:, :TILE]
            out_ref[q, cap : 2 * cap, :] = part[:, TILE:]
            out_ref[q, 2 * cap :, :] = jnp.zeros((INDEX_ROWS, TILE), BF)
            index = rows_ref[q : q + 1, :]
            value = jnp.where(sub == 0, index >> 7, jnp.where(sub == 1, index & (TILE - 1), 0))
            out_ref[q, 2 * cap :, 0:cap] = value.astype(F32).astype(BF)


def adjacency_kernel(src_ref, slot_ref, out_ref):
    verts, slots = out_ref.shape
    bins = verts // TILE
    repeats = src_ref.shape[1] // verts

    def one_bin(b, carry):
        source, blocks = bin_indicators(src_ref, slot_ref, b, bins, repeats, slots)
        row = pl.ds(pl.multiple_of(b * TILE, TILE), TILE)
        for h, block in enumerate(blocks):
            out_ref[row, h * TILE : (h + 1) * TILE] = dot(source, block, NT).astype(BF)
        return carry

    lax.fori_loop(0, bins, one_bin, 0)


def master_kernel(
    cap,
    ages_ref,
    got_ref,
    feats_ref,
    stale_ref,
    cot_ref,
    ws_ref,
    wn_ref,
    hidden_ref,
    gp_ref,
    out_ref,
    ga_ref,
    arr_ref,
):
    verts, width = feats_ref.shape
    peers = got_ref.shape[0]
    slots = peers * cap
    arr_ref[:, :TILE] = got_ref[:, 0:cap, :].reshape(slots, TILE)
    arr_ref[:, TILE:] = got_ref[:, cap : 2 * cap, :].reshape(slots, TILE)
    coded = got_ref[:, 2 * cap :, :].reshape(peers * INDEX_ROWS, TILE)
    pick_row = lax.broadcasted_iota(jnp.int32, (peers, peers * INDEX_ROWS), 1)
    pick_peer = lax.broadcasted_iota(jnp.int32, (peers, peers * INDEX_ROWS), 0) * INDEX_ROWS
    high = dot(mask(pick_row == pick_peer), coded, NN).astype(BF)
    low = dot(mask(pick_row == pick_peer + 1), coded, NN).astype(BF)
    slot = lax.broadcasted_iota(jnp.int32, (TILE, slots), 1)
    lane = lax.broadcasted_iota(jnp.int32, (TILE, slots), 0)
    spread = mask(slot % cap == lane)
    value = dot(high, spread, NN) * float(TILE) + dot(low, spread, NN)
    own = slot[:peers] // cap == lane[:peers]
    row_index = jnp.sum(jnp.where(own, value, 0.0), axis=0, keepdims=True).astype(jnp.int32)
    slot_c = lax.broadcasted_iota(jnp.int32, (slots, TILE), 0)
    lane_c = lax.broadcasted_iota(jnp.int32, (slots, TILE), 1)
    peer_c = mask(slot_c[:, :peers] // cap == lane_c[:, :peers])
    value_c = dot(peer_c, high, NN) * float(TILE) + dot(peer_c, low, NN)
    col_index = jnp.sum(
        jnp.where(slot_c % cap == lane_c, value_c, 0.0), axis=1, keepdims=True
    ).astype(jnp.int32)

    sub = lax.broadcasted_iota(jnp.int32, (TILE, slots), 0)
    low_hot = mask(sub == (row_index & (TILE - 1)))
    row_high = row_index >> 7
    total = None
    per = ROWS // TILE
    for block in range(verts // ROWS):
        rows = slice(block * ROWS, (block + 1) * ROWS)
        hot = jnp.concatenate(
            [low_hot * mask(row_high == block * per + k) for k in range(per)], axis=0
        )
        agg = dot(hot, arr_ref[...], NN)
        aged = jnp.concatenate(
            [
                stale_ref[(block * per + k) * TILE : (block * per + k + 1) * TILE, :].astype(F32)
                * ages_ref[block * per + k]
                for k in range(per)
            ],
            axis=0,
        )
        agg = agg + aged
        inverse = lax.rsqrt(jnp.mean(agg * agg, axis=1, keepdims=True) + 1e-05)
        normed = (agg * inverse).astype(BF)
        feats = feats_ref[rows, :]
        pre = dot(feats, ws_ref[...], NN) + dot(normed, wn_ref[...], NN)
        sig = jax.nn.sigmoid(pre)
        hidden_ref[rows, :] = (pre * sig).astype(BF)
        gp = (cot_ref[rows, :].astype(F32) * sig * (1.0 + pre * (1.0 - sig))).astype(BF)
        gp_ref[rows, :] = gp
        grads = jnp.concatenate([dot(feats, gp, TN), dot(normed, gp, TN)], axis=0)
        total = grads if total is None else total + grads
        gn = dot(gp, wn_ref[...], NT)
        inner = jnp.mean(gn * agg, axis=1, keepdims=True)
        ga_ref[rows, :] = (inverse * (gn - agg * (inverse * inverse * inner))).astype(BF)
    total = total.astype(BF)
    share = 2 * width // peers
    out_ref[:, 2 * cap : 2 * cap + share, :] = total[:, :TILE].reshape(peers, share, TILE)
    out_ref[:, 2 * cap + share :, :] = total[:, TILE:].reshape(peers, share, TILE)
    step = 8
    for first in range(0, peers, step):
        part = slice(first * cap, (first + step) * cap)
        lanes = lax.broadcasted_iota(jnp.int32, (step * cap, verts), 1)
        rows = dot(mask(lanes == col_index[part, :]), ga_ref[...], NN).astype(BF)
        out_ref[first : first + step, 0:cap, :] = rows[:, :TILE].reshape(step, cap, TILE)
        out_ref[first : first + step, cap : 2 * cap, :] = rows[:, TILE:].reshape(step, cap, TILE)


def back_kernel(cap, counts_ref, got_ref, adj_ref, gp_ref, ws_ref, out_ref, grad_ref):
    peers = got_ref.shape[0]
    slot_in_peer = lax.broadcasted_iota(jnp.int32, (cap, TILE), 0)
    for q in range(peers):
        live = slot_in_peer < counts_ref[0, q]
        for half in range(2):
            rows = got_ref[q, half * cap : (half + 1) * cap, :]
            grad_ref[q * cap : (q + 1) * cap, half * TILE : (half + 1) * TILE] = jnp.where(
                live, rows.astype(F32), 0.0
            ).astype(BF)
    for block in range(out_ref.shape[0] // ROWS):
        rows = slice(block * ROWS, (block + 1) * ROWS)
        out_ref[rows, :] = (
            dot(adj_ref[rows, :], grad_ref[...], NN) + dot(gp_ref[rows, :], ws_ref[...], NT)
        ).astype(BF)


def update_kernel(sum_ref, ws_ref, wn_ref, new_s_ref, new_n_ref):
    peers, share = sum_ref.shape[0], sum_ref.shape[1] // 2
    left = sum_ref[:, :share, :].astype(F32).reshape(peers * share, TILE)
    right = sum_ref[:, share:, :].astype(F32).reshape(peers * share, TILE)
    total = jnp.concatenate([left, right], axis=1)
    norm = jnp.sqrt(jnp.sum(total * total, keepdims=True))
    scale = 8.0 * jnp.minimum(1.0, 1.0 / norm)
    half = new_s_ref.shape[0]
    new_s_ref[...] = ws_ref[...].astype(F32) - scale * total[:half]
    new_n_ref[...] = wn_ref[...].astype(F32) - scale * total[half:]


SMEM = pl.BlockSpec(memory_space=pltpu.SMEM)
VMEM = pl.BlockSpec(memory_space=pltpu.VMEM)


def call(kernel, name, smem, args, outs, scratch=(), flops=10**9):
    size = sum(a.size * a.dtype.itemsize for a in args)
    return pl.pallas_call(
        kernel,
        name=name,
        in_specs=[SMEM] * smem + [VMEM] * (len(args) - smem),
        out_specs=[VMEM] * len(outs),
        out_shape=outs,
        scratch_shapes=list(scratch),
        compiler_params=pltpu.CompilerParams(vmem_limit_bytes=VMEM_BYTES),
        cost_estimate=pl.CostEstimate(flops=flops, bytes_accessed=size, transcendentals=0),
    )(*args)


def shape(dims, dtype=BF):
    return jax.ShapeDtypeStruct(dims, dtype)


def scatter(slot_counts, rows, edge_src, edge_slot, feats):
    peers, cap = rows.shape
    slots = peers * cap
    return call(
        scatter_kernel,
        "scatter",
        1,
        (slot_counts, rows, edge_src, edge_slot, feats),
        [shape((peers, 2 * cap + INDEX_ROWS, TILE))],
        [pltpu.VMEM((slots, feats.shape[0]), BF)],
    )[0]


def adjacency(edge_src, edge_slot, verts, slots):
    return call(
        adjacency_kernel, "adjacency", 0, (edge_src, edge_slot), [shape((verts, slots))], flops=6 * 10**9
    )[0]


def masters(cap, ages, got, feats, stale, cot, ws, wn):
    verts, width = feats.shape
    peers = got.shape[0]
    share = 2 * width // peers
    return call(
        functools.partial(master_kernel, cap),
        "masters",
        1,
        (ages, got, feats, stale, cot, ws, wn),
        [shape((verts, width)), shape((verts, width)), shape((peers, 2 * cap + 2 * share, TILE))],
        [pltpu.VMEM((verts, width), BF), pltpu.VMEM((peers * cap, width), BF)],
    )


def back(cap, slot_counts, got, adj, gp, ws):
    return call(
        functools.partial(back_kernel, cap),
        "back",
        1,
        (slot_counts, got, adj, gp, ws),
        [shape(gp.shape)],
        [pltpu.VMEM((got.shape[0] * cap, gp.shape[1]), BF)],
    )[0]


def update(sums, ws, wn):
    return call(update_kernel, "update", 0, (sums, ws, wn), [shape(ws.shape, F32)] * 2)


def exchange(x):
    return lax.all_to_all(x, "dom", split_axis=0, concat_axis=0, tiled=True)


def body(
    feats, edge_src, edge_slot, slot_counts, replica_row, stale_agg, bin_ages, cotangent, w_self, w_neigh
):
    verts, width = feats.shape
    peers, cap = replica_row.shape[1:]
    arrived = exchange(scatter(slot_counts, replica_row[0], edge_src, edge_slot, feats))
    adj = adjacency(edge_src, edge_slot, verts, peers * cap)
    age_factor = 1.0 / (1.0 + bin_ages.astype(F32))
    hidden, grad_pre, outgoing = masters(
        cap, age_factor, arrived, feats, stale_agg, cotangent, w_self, w_neigh
    )
    returned = exchange(outgoing)
    partial = jnp.sum(returned[:, 2 * cap :, :].astype(F32), axis=0)
    groups = lax.axis_size("group")
    if groups & (groups - 1):
        partial = lax.psum(partial, "group")
    else:
        step = 1
        while step < groups:
            pairs = [(k, k ^ (2 * step - 1)) for k in range(groups)]
            partial = partial + lax.ppermute(partial, "group", pairs)
            step *= 2
    share = partial.astype(BF)
    sums = exchange(jnp.broadcast_to(share[None], (peers,) + share.shape))
    feat_grad = back(cap, slot_counts, returned, adj, grad_pre, w_self)
    new_self, new_neigh = update(sums, w_self, w_neigh)
    return (hidden, feat_grad, new_self, new_neigh)


def solution(mesh):
    both = ("group", "dom")
    wide = P(both, None)
    placed = (wide, wide, wide, wide, P(both, None, None), wide, P(both), wide, P(), P())
    return jax.shard_map(
        body,
        mesh=mesh,
        in_specs=placed,
        out_specs=(wide, wide, P(), P()),
        check_vma=False,
    )
```

```python
import functools

import jax
import jax.numpy as jnp
from jax import lax
from jax.experimental import pallas as pl
from jax.experimental.pallas import tpu as pltpu
from jax.sharding import PartitionSpec as P

BF = jnp.bfloat16
F8 = jnp.float8_e4m3fn
F32 = jnp.float32
TILE = 128
ROWS = 512
INDEX_ROWS = 16
NN = (((1,), (0,)), ((), ()))
NT = (((1,), (1,)), ((), ()))
TN = (((0,), (0,)), ((), ()))
MIB = 1024 * 1024


def dot(a, b, dims):
    return lax.dot_general(a, b, dims, preferred_element_type=F32)


def mask(cond):
    return jnp.where(cond, 1.0, 0.0).astype(BF)


def start_all(pairs, sems):
    copies = [pltpu.make_async_copy(src, dst, sems.at[k]) for k, (src, dst) in enumerate(pairs)]
    for copy in copies:
        copy.start()
    return copies


def bin_edges(ref, b, bins, repeats):
    return jnp.concatenate(
        [ref[:, (g * bins + b) * TILE : (g * bins + b + 1) * TILE] for g in range(repeats)], axis=1
    )


def bin_indicators(src_ref, slot_ref, b, bins, repeats, slots):
    src = bin_edges(src_ref, b, bins, repeats) & (TILE - 1)
    slot = bin_edges(slot_ref, b, bins, repeats)
    row = lax.broadcasted_iota(jnp.int32, (TILE, src.shape[1]), 0)
    source = mask(row == src).astype(F8)
    low = mask(row == (slot & (TILE - 1)))
    high = slot >> 7
    return source, [(low * mask(high == h)).astype(F8) for h in range(slots // TILE)]


def scatter_kernel(
    counts_hbm, rows_hbm, src_hbm, slot_hbm, feats_hbm, out_ref, adj_ref, counts_ref, rows_ref, src_ref, slot_ref, feats_ref, sems
):
    copies = start_all(
        [
            (src_hbm, src_ref),
            (slot_hbm, slot_ref),
            (feats_hbm, feats_ref),
            (rows_hbm, rows_ref),
            (counts_hbm, counts_ref),
        ],
        sems,
    )
    slots, verts = adj_ref.shape
    peers, cap = rows_ref.shape[1:]
    bins = verts // TILE
    repeats = src_ref.shape[1] // verts
    copies[0].wait()
    copies[1].wait()
    for b in range(bins):
        source, blocks = bin_indicators(src_ref, slot_ref, b, bins, repeats, slots)
        for h, block in enumerate(blocks):
            adj_ref[h * TILE : (h + 1) * TILE, b * TILE : (b + 1) * TILE] = dot(block, source, NT).astype(BF)
    for copy in copies[2:]:
        copy.wait()
    sub = lax.broadcasted_iota(jnp.int32, (INDEX_ROWS, cap), 0)
    slot_in_peer = lax.broadcasted_iota(jnp.int32, (cap, 2 * TILE), 0)
    step = 8
    for first in range(0, peers, step):
        rows = dot(adj_ref[first * cap : (first + step) * cap, :], feats_ref[...], NN)
        for q in range(first, first + step):
            part = rows[(q - first) * cap : (q - first + 1) * cap, :]
            part = jnp.where(slot_in_peer < counts_ref[0, q], part, 0.0).astype(BF)
            out_ref[q, 0:cap, :] = part[:, :TILE]
            out_ref[q, cap : 2 * cap, :] = part[:, TILE:]
            out_ref[q, 2 * cap :, :] = jnp.zeros((INDEX_ROWS, TILE), BF)
            index = rows_ref[0, q : q + 1, :]
            value = jnp.where(sub == 0, index >> 7, jnp.where(sub == 1, index & (TILE - 1), 0))
            out_ref[q, 2 * cap :, 0:cap] = value.astype(F32).astype(BF)


def adjacency_kernel(src_hbm, slot_hbm, out_hbm, src_ref, slot_ref, adj_ref, sems, out_sems):
    copies = start_all([(src_hbm, src_ref), (slot_hbm, slot_ref)], sems)
    verts, slots = adj_ref.shape
    bins = verts // TILE
    repeats = src_ref.shape[1] // verts
    for copy in copies:
        copy.wait()
    outs = []
    per = ROWS // TILE
    for b in range(bins):
        source, blocks = bin_indicators(src_ref, slot_ref, b, bins, repeats, slots)
        for h, block in enumerate(blocks):
            adj_ref[b * TILE : (b + 1) * TILE, h * TILE : (h + 1) * TILE] = dot(source, block, NT).astype(BF)
        if b % per == per - 1:
            rows = pl.ds((b // per) * ROWS, ROWS)
            copy = pltpu.make_async_copy(adj_ref.at[rows], out_hbm.at[rows], out_sems.at[b // per])
            copy.start()
            outs.append(copy)
    for copy in outs:
        copy.wait()


def master_kernel(
    cap,
    got_ref,
    adj_hbm,
    ages_hbm,
    feats_hbm,
    stale_hbm,
    cot_hbm,
    ws_hbm,
    wn_hbm,
    hidden_hbm,
    gp_ref,
    out_ref,
    ages_ref,
    feats_ref,
    stale_ref,
    cot_ref,
    ws_ref,
    wn_ref,
    hidden_ref,
    ga_ref,
    arr_ref,
    sems,
    out_sems,
):
    copies = start_all(
        [
            (ages_hbm, ages_ref),
            (stale_hbm, stale_ref),
            (feats_hbm, feats_ref),
            (ws_hbm, ws_ref),
            (wn_hbm, wn_ref),
            (cot_hbm, cot_ref),
        ],
        sems,
    )
    verts, width = feats_ref.shape
    peers = got_ref.shape[0]
    slots = peers * cap
    arr_ref[:, :TILE] = got_ref[:, 0:cap, :].reshape(slots, TILE)
    arr_ref[:, TILE:] = got_ref[:, cap : 2 * cap, :].reshape(slots, TILE)
    coded = got_ref[:, 2 * cap :, :].reshape(peers * INDEX_ROWS, TILE)
    pick_row = lax.broadcasted_iota(jnp.int32, (peers, peers * INDEX_ROWS), 1)
    pick_peer = lax.broadcasted_iota(jnp.int32, (peers, peers * INDEX_ROWS), 0) * INDEX_ROWS
    high = dot(mask(pick_row == pick_peer), coded, NN).astype(BF)
    low = dot(mask(pick_row == pick_peer + 1), coded, NN).astype(BF)
    place = lax.broadcasted_iota(jnp.int32, (peers, cap, TILE), 1).reshape(slots, TILE)
    peer = lax.broadcasted_iota(jnp.int32, (peers, cap, TILE), 0).reshape(slots, TILE)
    lane = lax.broadcasted_iota(jnp.int32, (slots, TILE), 1)
    at_place = place == lane
    at_peer = mask(peer == lane)[:, :peers]
    value_c = dot(at_peer, high, NN) * float(TILE) + dot(at_peer, low, NN)
    col_index = jnp.sum(jnp.where(at_place, value_c, 0.0), axis=1, keepdims=True).astype(jnp.int32)
    spread = mask(at_place)
    value = dot(high, spread, NT) * float(TILE) + dot(low, spread, NT)
    slot = lax.broadcasted_iota(jnp.int32, (peers, slots), 1)
    least = lax.broadcasted_iota(jnp.int32, (peers, slots), 0) * cap
    own = (slot >= least) & (slot < least + cap)
    row_index = jnp.sum(jnp.where(own, value, 0.0), axis=0, keepdims=True).astype(jnp.int32)

    sub = lax.broadcasted_iota(jnp.int32, (TILE, slots), 0)
    low_hot = mask(sub == (row_index & (TILE - 1)))
    row_high = row_index >> 7
    total = None
    outs = []
    per = ROWS // TILE
    for block in range(verts // ROWS):
        rows = slice(block * ROWS, (block + 1) * ROWS)
        hot = jnp.concatenate([low_hot * mask(row_high == block * per + k) for k in range(per)], axis=0)
        agg = dot(hot, arr_ref[...], NN)
        if block == 0:
            copies[0].wait()
            copies[1].wait()
        aged = []
        for k in range(block * per, (block + 1) * per):
            age = jnp.full((1, width), ages_ref[k], jnp.int32).astype(F32)
            aged.append(stale_ref[k * TILE : (k + 1) * TILE, :].astype(F32) * (1.0 / (1.0 + age)))
        agg = agg + jnp.concatenate(aged, axis=0)
        inverse = lax.rsqrt(jnp.mean(agg * agg, axis=1, keepdims=True) + 1e-05)
        normed = (agg * inverse).astype(BF)
        if block == 0:
            for copy in copies[2:]:
                copy.wait()
        feats = feats_ref[rows, :]
        pre = dot(feats, ws_ref[...], NN) + dot(normed, wn_ref[...], NN)
        sig = jax.nn.sigmoid(pre)
        hidden_ref[rows, :] = (pre * sig).astype(BF)
        gp = (cot_ref[rows, :].astype(F32) * sig * (1.0 + pre * (1.0 - sig))).astype(BF)
        gp_ref[rows, :] = gp
        part = pl.ds(block * ROWS, ROWS)
        copy = pltpu.make_async_copy(hidden_ref.at[part], hidden_hbm.at[part], out_sems.at[block])
        copy.start()
        outs.append(copy)
        grads = jnp.concatenate([dot(feats, gp, TN), dot(normed, gp, TN)], axis=0)
        total = grads if total is None else total + grads
        gn = dot(gp, wn_ref[...], NT)
        inner = jnp.mean(gn * agg, axis=1, keepdims=True)
        ga_ref[rows, :] = (inverse * (gn - agg * (inverse * inverse * inner))).astype(BF)
    total = total.astype(BF)
    share = 2 * width // peers
    out_ref[:, 2 * cap : 2 * cap + share, :] = total[:, :TILE].reshape(peers, share, TILE)
    out_ref[:, 2 * cap + share :, :] = total[:, TILE:].reshape(peers, share, TILE)
    step = 8
    for first in range(0, peers, step):
        part = slice(first * cap, (first + step) * cap)
        lanes = lax.broadcasted_iota(jnp.int32, (step * cap, verts), 1)
        rows = dot(mask(lanes == col_index[part, :]), ga_ref[...], NN).astype(BF)
        out_ref[first : first + step, 0:cap, :] = rows[:, :TILE].reshape(step, cap, TILE)
        out_ref[first : first + step, cap : 2 * cap, :] = rows[:, TILE:].reshape(step, cap, TILE)
    for copy in outs:
        copy.wait()


def back_kernel(cap, got_ref, gp_ref, counts_hbm, adj_hbm, ws_hbm, out_hbm, counts_ref, adj_ref, ws_ref, grad_ref, out_ref, sems, out_sems):
    verts = out_ref.shape[0]
    blocks = verts // ROWS
    pairs = [(counts_hbm, counts_ref), (ws_hbm, ws_ref)]
    for block in range(blocks):
        part = pl.ds(block * ROWS, ROWS)
        pairs.append((adj_hbm.at[part], adj_ref.at[part]))
    copies = start_all(pairs, sems)
    peers = got_ref.shape[0]
    copies[0].wait()
    copies[1].wait()
    slot_in_peer = lax.broadcasted_iota(jnp.int32, (cap, TILE), 0)
    for q in range(peers):
        live = slot_in_peer < counts_ref[0, q]
        for half in range(2):
            rows = got_ref[q, half * cap : (half + 1) * cap, :]
            grad_ref[q * cap : (q + 1) * cap, half * TILE : (half + 1) * TILE] = jnp.where(
                live, rows.astype(F32), 0.0
            ).astype(BF)
    outs = []
    for block in range(blocks):
        rows = slice(block * ROWS, (block + 1) * ROWS)
        own = dot(gp_ref[rows, :], ws_ref[...], NT)
        copies[2 + block].wait()
        out_ref[rows, :] = (dot(adj_ref[rows, :], grad_ref[...], NN) + own).astype(BF)
        part = pl.ds(block * ROWS, ROWS)
        copy = pltpu.make_async_copy(out_ref.at[part], out_hbm.at[part], out_sems.at[block])
        copy.start()
        outs.append(copy)
    for copy in outs:
        copy.wait()


def update_kernel(sum_ref, ws_ref, wn_ref, new_s_ref, new_n_ref):
    peers, share = sum_ref.shape[0], sum_ref.shape[1] // 2
    left = sum_ref[:, :share, :].astype(F32).reshape(peers * share, TILE)
    right = sum_ref[:, share:, :].astype(F32).reshape(peers * share, TILE)
    total = jnp.concatenate([left, right], axis=1)
    norm = jnp.sqrt(jnp.sum(total * total, keepdims=True))
    scale = 8.0 * jnp.minimum(1.0, 1.0 / norm)
    half = new_s_ref.shape[0]
    new_s_ref[...] = ws_ref[...].astype(F32) - scale * total[:half]
    new_n_ref[...] = wn_ref[...].astype(F32) - scale * total[half:]


HBM = pl.BlockSpec(memory_space=pltpu.HBM)
VMEM = pl.BlockSpec(memory_space=pltpu.VMEM)


def call(kernel, name, args, near, outs, out_near, scratch=(), flops=10**9, limit=56):
    size = sum(a.size * a.dtype.itemsize for a in args)
    return pl.pallas_call(
        kernel,
        name=name,
        in_specs=[VMEM if k < near else HBM for k in range(len(args))],
        out_specs=[VMEM if k in out_near else HBM for k in range(len(outs))],
        out_shape=outs,
        scratch_shapes=list(scratch),
        compiler_params=pltpu.CompilerParams(vmem_limit_bytes=limit * MIB),
        cost_estimate=pl.CostEstimate(flops=flops, bytes_accessed=size, transcendentals=0),
    )(*args)


def shape(dims, dtype=BF):
    return jax.ShapeDtypeStruct(dims, dtype)


def like(x):
    return pltpu.VMEM(x.shape, x.dtype)


def scatter(slot_counts, replica_row, edge_src, edge_slot, feats):
    peers, cap = replica_row.shape[1:]
    return call(
        scatter_kernel,
        "scatter",
        (slot_counts, replica_row, edge_src, edge_slot, feats),
        0,
        [shape((peers, 2 * cap + INDEX_ROWS, TILE))],
        (0,),
        [
            pltpu.VMEM((peers * cap, feats.shape[0]), BF),
            pltpu.SMEM(slot_counts.shape, jnp.int32),
            like(replica_row),
            like(edge_src),
            like(edge_slot),
            like(feats),
            pltpu.SemaphoreType.DMA((5,)),
        ],
    )[0]


def adjacency(edge_src, edge_slot, verts, slots):
    return call(
        adjacency_kernel,
        "adjacency",
        (edge_src, edge_slot),
        0,
        [shape((verts, slots))],
        (),
        [
            like(edge_src),
            like(edge_slot),
            pltpu.VMEM((verts, slots), BF),
            pltpu.SemaphoreType.DMA((2,)),
            pltpu.SemaphoreType.DMA((verts // ROWS,)),
        ],
        flops=6 * 10**9,
    )[0]


def masters(cap, got, adj, ages, feats, stale, cot, ws, wn):
    verts, width = feats.shape
    peers = got.shape[0]
    share = 2 * width // peers
    return call(
        functools.partial(master_kernel, cap),
        "masters",
        (got, adj, ages, feats, stale, cot, ws, wn),
        1,
        [shape((verts, width)), shape((verts, width)), shape((peers, 2 * cap + 2 * share, TILE))],
        (1, 2),
        [
            pltpu.SMEM(ages.shape, jnp.int32),
            like(feats),
            like(stale),
            like(cot),
            like(ws),
            like(wn),
            like(feats),
            like(feats),
            pltpu.VMEM((peers * cap, width), BF),
            pltpu.SemaphoreType.DMA((6,)),
            pltpu.SemaphoreType.DMA((verts // ROWS,)),
        ],
    )


def back(cap, got, gp, slot_counts, adj, ws):
    blocks = gp.shape[0] // ROWS
    return call(
        functools.partial(back_kernel, cap),
        "back",
        (got, gp, slot_counts, adj, ws),
        2,
        [shape(gp.shape)],
        (),
        [
            pltpu.SMEM(slot_counts.shape, jnp.int32),
            like(adj),
            like(ws),
            pltpu.VMEM((got.shape[0] * cap, gp.shape[1]), BF),
            like(gp),
            pltpu.SemaphoreType.DMA((2 + blocks,)),
            pltpu.SemaphoreType.DMA((blocks,)),
        ],
    )[0]


def update(sums, ws, wn):
    return call(update_kernel, "update", (sums, ws, wn), 3, [shape(ws.shape, F32)] * 2, (0, 1))


def exchange(x):
    return lax.all_to_all(x, "dom", split_axis=0, concat_axis=0, tiled=True)


def body(
    feats, edge_src, edge_slot, slot_counts, replica_row, stale_agg, bin_ages, cotangent, w_self, w_neigh
):
    verts, width = feats.shape
    peers, cap = replica_row.shape[1:]
    arrived = exchange(scatter(slot_counts, replica_row, edge_src, edge_slot, feats))
    adj = adjacency(edge_src, edge_slot, verts, peers * cap)
    hidden, grad_pre, outgoing = masters(
        cap, arrived, adj, bin_ages, feats, stale_agg, cotangent, w_self, w_neigh
    )
    returned = exchange(outgoing)
    partial = jnp.sum(returned[:, 2 * cap :, :].astype(F32), axis=0)
    groups = lax.axis_size("group")
    step = 1
    while step < groups:
        pairs = [(k, k ^ (2 * step - 1)) for k in range(groups)]
        partial = partial + lax.ppermute(partial, "group", pairs)
        step *= 2
    share = partial.astype(BF)
    sums = exchange(jnp.broadcast_to(share[None], (peers,) + share.shape))
    feat_grad = back(cap, returned, grad_pre, slot_counts, adj, w_self)
    new_self, new_neigh = update(sums, w_self, w_neigh)
    return (hidden, feat_grad, new_self, new_neigh)


def solution(mesh):
    both = ("group", "dom")
    wide = P(both, None)
    placed = (wide, wide, wide, wide, P(both, None, None), wide, P(both), wide, P(), P())
    return jax.shard_map(
        body,
        mesh=mesh,
        in_specs=placed,
        out_specs=(wide, wide, P(), P()),
        check_vma=False,
    )
```

```python
import functools

import jax
import jax.numpy as jnp
from jax import lax
from jax.experimental import pallas as pl
from jax.experimental.pallas import tpu as pltpu
from jax.sharding import PartitionSpec as P

BF = jnp.bfloat16
F8 = jnp.float8_e4m3fn
F32 = jnp.float32
TILE = 128
ROWS = 512
INDEX_ROWS = 16
GATHER_STEPS = 4
NN = (((1,), (0,)), ((), ()))
NT = (((1,), (1,)), ((), ()))
TN = (((0,), (0,)), ((), ()))
MIB = 1024 * 1024


def dot(a, b, dims):
    return lax.dot_general(a, b, dims, preferred_element_type=F32)


def mask(cond):
    return jnp.where(cond, 1.0, 0.0).astype(BF)


def start_all(pairs, sems):
    copies = [pltpu.make_async_copy(src, dst, sems.at[k]) for k, (src, dst) in enumerate(pairs)]
    for copy in copies:
        copy.start()
    return copies


def bin_edges(ref, b, bins, repeats):
    return jnp.concatenate(
        [ref[:, (g * bins + b) * TILE : (g * bins + b + 1) * TILE] for g in range(repeats)], axis=1
    )


def bin_indicators(src_ref, slot_ref, b, bins, repeats, slots):
    src = bin_edges(src_ref, b, bins, repeats) & (TILE - 1)
    slot = bin_edges(slot_ref, b, bins, repeats)
    row = lax.broadcasted_iota(jnp.int32, (TILE, src.shape[1]), 0)
    source = mask(row == src).astype(F8)
    low = mask(row == (slot & (TILE - 1)))
    high = slot >> 7
    return source, [(low * mask(high == h)).astype(F8) for h in range(slots // TILE)]


def scatter_kernel(
    counts_hbm, rows_hbm, src_hbm, slot_hbm, feats_hbm, out_hbm, out_ref, adj_ref, counts_ref, rows_ref, src_ref, slot_ref, feats_ref, sems, out_sems
):
    copies = start_all(
        [
            (src_hbm, src_ref),
            (slot_hbm, slot_ref),
            (feats_hbm, feats_ref),
            (rows_hbm, rows_ref),
            (counts_hbm, counts_ref),
        ],
        sems,
    )
    slots, verts = adj_ref.shape
    peers, cap = rows_ref.shape[1:]
    bins = verts // TILE
    repeats = src_ref.shape[1] // verts
    copies[0].wait()
    copies[1].wait()
    for b in range(bins):
        source, blocks = bin_indicators(src_ref, slot_ref, b, bins, repeats, slots)
        for h, block in enumerate(blocks):
            adj_ref[h * TILE : (h + 1) * TILE, b * TILE : (b + 1) * TILE] = dot(block, source, NT).astype(BF)
    for copy in copies[2:]:
        copy.wait()
    sub = lax.broadcasted_iota(jnp.int32, (INDEX_ROWS, cap), 0)
    slot_in_peer = lax.broadcasted_iota(jnp.int32, (cap, 2 * TILE), 0)
    outs = []
    step = peers // GATHER_STEPS
    for first in range(0, peers, step):
        rows = dot(adj_ref[first * cap : (first + step) * cap, :], feats_ref[...], NN)
        for q in range(first, first + step):
            part = rows[(q - first) * cap : (q - first + 1) * cap, :]
            part = jnp.where(slot_in_peer < counts_ref[0, q], part, 0.0).astype(BF)
            out_ref[q, 0:cap, :] = part[:, :TILE]
            out_ref[q, cap : 2 * cap, :] = part[:, TILE:]
            out_ref[q, 2 * cap :, :] = jnp.zeros((INDEX_ROWS, TILE), BF)
            index = rows_ref[0, q : q + 1, :]
            value = jnp.where(sub == 0, index >> 7, jnp.where(sub == 1, index & (TILE - 1), 0))
            out_ref[q, 2 * cap :, 0:cap] = value.astype(F32).astype(BF)
        those = pl.ds(first, step)
        copy = pltpu.make_async_copy(out_ref.at[those], out_hbm.at[those], out_sems.at[first // step])
        copy.start()
        outs.append(copy)
    for copy in outs:
        copy.wait()


def adjacency_kernel(src_hbm, slot_hbm, out_hbm, src_ref, slot_ref, adj_ref, sems, out_sems):
    copies = start_all([(src_hbm, src_ref), (slot_hbm, slot_ref)], sems)
    verts, slots = adj_ref.shape
    bins = verts // TILE
    repeats = src_ref.shape[1] // verts
    for copy in copies:
        copy.wait()
    outs = []
    per = ROWS // TILE
    for b in range(bins):
        source, blocks = bin_indicators(src_ref, slot_ref, b, bins, repeats, slots)
        for h, block in enumerate(blocks):
            adj_ref[b * TILE : (b + 1) * TILE, h * TILE : (h + 1) * TILE] = dot(source, block, NT).astype(BF)
        if b % per == per - 1:
            rows = pl.ds((b // per) * ROWS, ROWS)
            copy = pltpu.make_async_copy(adj_ref.at[rows], out_hbm.at[rows], out_sems.at[b // per])
            copy.start()
            outs.append(copy)
    for copy in outs:
        copy.wait()


def master_kernel(
    cap,
    got_hbm,
    adj_hbm,
    ages_hbm,
    feats_hbm,
    stale_hbm,
    cot_hbm,
    ws_hbm,
    wn_hbm,
    hidden_hbm,
    gp_hbm,
    out_hbm,
    arr_ref,
    coded_ref,
    ages_ref,
    feats_ref,
    stale_ref,
    cot_ref,
    ws_ref,
    wn_ref,
    hidden_ref,
    gp_ref,
    ga_ref,
    back_ref,
    share_ref,
    agg_ref,
    sems,
    out_sems,
):
    peers = arr_ref.shape[0]
    verts, width = feats_ref.shape
    slots = peers * cap
    blocks = verts // ROWS
    copies = start_all(
        [
            (got_hbm.at[:, pl.ds(2 * cap, INDEX_ROWS), :], coded_ref),
            (got_hbm.at[:, pl.ds(0, cap), :], arr_ref.at[:, :, pl.ds(0, TILE)]),
            (got_hbm.at[:, pl.ds(cap, cap), :], arr_ref.at[:, :, pl.ds(TILE, TILE)]),
            (ages_hbm, ages_ref),
            (stale_hbm, stale_ref),
            (feats_hbm, feats_ref),
            (ws_hbm, ws_ref),
            (wn_hbm, wn_ref),
            (cot_hbm, cot_ref),
        ],
        sems,
    )
    copies[0].wait()
    coded = coded_ref[...].reshape(peers * INDEX_ROWS, TILE)
    pick_row = lax.broadcasted_iota(jnp.int32, (peers, peers * INDEX_ROWS), 1)
    pick_peer = lax.broadcasted_iota(jnp.int32, (peers, peers * INDEX_ROWS), 0) * INDEX_ROWS
    high = dot(mask(pick_row == pick_peer), coded, NN).astype(BF)
    low = dot(mask(pick_row == pick_peer + 1), coded, NN).astype(BF)
    place = lax.broadcasted_iota(jnp.int32, (peers, cap, TILE), 1).reshape(slots, TILE)
    peer = lax.broadcasted_iota(jnp.int32, (peers, cap, TILE), 0).reshape(slots, TILE)
    lane = lax.broadcasted_iota(jnp.int32, (slots, TILE), 1)
    at_place = place == lane
    spread = mask(at_place)
    value = dot(high, spread, NT) * float(TILE) + dot(low, spread, NT)
    slot = lax.broadcasted_iota(jnp.int32, (peers, slots), 1)
    least = lax.broadcasted_iota(jnp.int32, (peers, slots), 0) * cap
    own = (slot >= least) & (slot < least + cap)
    row_index = jnp.sum(jnp.where(own, value, 0.0), axis=0, keepdims=True).astype(jnp.int32)
    sub = lax.broadcasted_iota(jnp.int32, (TILE, slots), 0)
    low_hot = mask(sub == (row_index & (TILE - 1)))
    row_high = row_index >> 7
    at_peer = mask(peer == lane)[:, :peers]
    value_c = dot(at_peer, high, NN) * float(TILE) + dot(at_peer, low, NN)
    col_index = jnp.sum(jnp.where(at_place, value_c, 0.0), axis=1, keepdims=True).astype(jnp.int32)
    for copy in copies[1:3]:
        copy.wait()
    total = None
    outs = []
    per = ROWS // TILE

    def send(src, dst):
        copy = pltpu.make_async_copy(src, dst, out_sems.at[len(outs)])
        copy.start()
        outs.append(copy)

    for block in range(blocks):
        hot = jnp.concatenate([low_hot * mask(row_high == block * per + k) for k in range(per)], axis=0)
        agg_ref[block * ROWS : (block + 1) * ROWS, :] = dot(hot, arr_ref[...].reshape(slots, width), NN)
    for block in range(blocks):
        rows = slice(block * ROWS, (block + 1) * ROWS)
        agg = agg_ref[rows, :]
        if block == 0:
            copies[3].wait()
            copies[4].wait()
        aged = []
        for k in range(block * per, (block + 1) * per):
            age = jnp.full((1, width), ages_ref[k], jnp.int32).astype(F32)
            aged.append(stale_ref[k * TILE : (k + 1) * TILE, :].astype(F32) * (1.0 / (1.0 + age)))
        agg = agg + jnp.concatenate(aged, axis=0)
        inverse = lax.rsqrt(jnp.mean(agg * agg, axis=1, keepdims=True) + 1e-05)
        normed = (agg * inverse).astype(BF)
        if block == 0:
            for copy in copies[5:]:
                copy.wait()
        feats = feats_ref[rows, :]
        pre = dot(feats, ws_ref[...], NN) + dot(normed, wn_ref[...], NN)
        sig = jax.nn.sigmoid(pre)
        hidden_ref[rows, :] = (pre * sig).astype(BF)
        gp = (cot_ref[rows, :].astype(F32) * sig * (1.0 + pre * (1.0 - sig))).astype(BF)
        gp_ref[rows, :] = gp
        part = pl.ds(block * ROWS, ROWS)
        send(hidden_ref.at[part], hidden_hbm.at[part])
        send(gp_ref.at[part], gp_hbm.at[part])
        grads = jnp.concatenate([dot(feats, gp, TN), dot(normed, gp, TN)], axis=0)
        total = grads if total is None else total + grads
        gn = dot(gp, wn_ref[...], NT)
        inner = jnp.mean(gn * agg, axis=1, keepdims=True)
        ga_ref[rows, :] = (inverse * (gn - agg * (inverse * inverse * inner))).astype(BF)
    total = total.astype(BF)
    share = 2 * width // peers
    share_ref[:, :share, :] = total[:, :TILE].reshape(peers, share, TILE)
    share_ref[:, share:, :] = total[:, TILE:].reshape(peers, share, TILE)
    send(share_ref, out_hbm.at[:, pl.ds(2 * cap, 2 * share), :])
    step = peers // GATHER_STEPS
    for first in range(0, peers, step):
        part = slice(first * cap, (first + step) * cap)
        lanes = lax.broadcasted_iota(jnp.int32, (step * cap, verts), 1)
        rows = dot(mask(lanes == col_index[part, :]), ga_ref[...], NN).astype(BF)
        back_ref[first : first + step, 0:cap, :] = rows[:, :TILE].reshape(step, cap, TILE)
        back_ref[first : first + step, cap:, :] = rows[:, TILE:].reshape(step, cap, TILE)
        those = pl.ds(first, step)
        send(back_ref.at[those], out_hbm.at[those, pl.ds(0, 2 * cap), :])
    for copy in outs:
        copy.wait()


def back_kernel(
    cap, got_hbm, gp_hbm, counts_hbm, adj_hbm, ws_hbm, out_hbm, got_ref, gp_ref, counts_ref, adj_ref, ws_ref, grad_ref, out_ref, sems, out_sems
):
    verts = out_ref.shape[0]
    blocks = verts // ROWS
    pairs = [
        (counts_hbm, counts_ref),
        (got_hbm.at[:, pl.ds(0, 2 * cap), :], got_ref),
        (ws_hbm, ws_ref),
        (gp_hbm, gp_ref),
    ]
    for block in range(blocks):
        part = pl.ds(block * ROWS, ROWS)
        pairs.append((adj_hbm.at[part], adj_ref.at[part]))
    copies = start_all(pairs, sems)
    peers = got_ref.shape[0]
    copies[0].wait()
    copies[1].wait()
    slot_in_peer = lax.broadcasted_iota(jnp.int32, (cap, TILE), 0)
    for q in range(peers):
        live = slot_in_peer < counts_ref[0, q]
        for half in range(2):
            rows = got_ref[q, half * cap : (half + 1) * cap, :]
            grad_ref[q * cap : (q + 1) * cap, half * TILE : (half + 1) * TILE] = jnp.where(
                live, rows.astype(F32), 0.0
            ).astype(BF)
    outs = []
    copies[2].wait()
    copies[3].wait()
    for block in range(blocks):
        rows = slice(block * ROWS, (block + 1) * ROWS)
        own = dot(gp_ref[rows, :], ws_ref[...], NT)
        copies[4 + block].wait()
        out_ref[rows, :] = (dot(adj_ref[rows, :], grad_ref[...], NN) + own).astype(BF)
        part = pl.ds(block * ROWS, ROWS)
        copy = pltpu.make_async_copy(out_ref.at[part], out_hbm.at[part], out_sems.at[block])
        copy.start()
        outs.append(copy)
    for copy in outs:
        copy.wait()


def update_kernel(sum_ref, ws_ref, wn_ref, new_s_ref, new_n_ref):
    peers, share = sum_ref.shape[0], sum_ref.shape[1] // 2
    left = sum_ref[:, :share, :].astype(F32).reshape(peers * share, TILE)
    right = sum_ref[:, share:, :].astype(F32).reshape(peers * share, TILE)
    total = jnp.concatenate([left, right], axis=1)
    norm = jnp.sqrt(jnp.sum(total * total, keepdims=True))
    scale = 8.0 * jnp.minimum(1.0, 1.0 / norm)
    half = new_s_ref.shape[0]
    new_s_ref[...] = ws_ref[...].astype(F32) - scale * total[:half]
    new_n_ref[...] = wn_ref[...].astype(F32) - scale * total[half:]


HBM = pl.BlockSpec(memory_space=pltpu.HBM)
VMEM = pl.BlockSpec(memory_space=pltpu.VMEM)


def call(kernel, name, args, near, outs, out_near, scratch=(), flops=10**9, limit=56):
    size = sum(a.size * a.dtype.itemsize for a in args)
    return pl.pallas_call(
        kernel,
        name=name,
        in_specs=[VMEM if k < near else HBM for k in range(len(args))],
        out_specs=[VMEM if k in out_near else HBM for k in range(len(outs))],
        out_shape=outs,
        scratch_shapes=list(scratch),
        compiler_params=pltpu.CompilerParams(vmem_limit_bytes=limit * MIB),
        cost_estimate=pl.CostEstimate(flops=flops, bytes_accessed=size, transcendentals=0),
    )(*args)


def shape(dims, dtype=BF):
    return jax.ShapeDtypeStruct(dims, dtype)


def like(x):
    return pltpu.VMEM(x.shape, x.dtype)


def scatter(slot_counts, replica_row, edge_src, edge_slot, feats):
    peers, cap = replica_row.shape[1:]
    return call(
        scatter_kernel,
        "scatter",
        (slot_counts, replica_row, edge_src, edge_slot, feats),
        0,
        [shape((peers, 2 * cap + INDEX_ROWS, TILE))],
        (),
        [
            pltpu.VMEM((peers, 2 * cap + INDEX_ROWS, TILE), BF),
            pltpu.VMEM((peers * cap, feats.shape[0]), BF),
            pltpu.SMEM(slot_counts.shape, jnp.int32),
            like(replica_row),
            like(edge_src),
            like(edge_slot),
            like(feats),
            pltpu.SemaphoreType.DMA((5,)),
            pltpu.SemaphoreType.DMA((GATHER_STEPS,)),
        ],
    )[0]


def adjacency(edge_src, edge_slot, verts, slots):
    return call(
        adjacency_kernel,
        "adjacency",
        (edge_src, edge_slot),
        0,
        [shape((verts, slots))],
        (),
        [
            like(edge_src),
            like(edge_slot),
            pltpu.VMEM((verts, slots), BF),
            pltpu.SemaphoreType.DMA((2,)),
            pltpu.SemaphoreType.DMA((verts // ROWS,)),
        ],
        flops=6 * 10**9,
    )[0]


def masters(cap, got, adj, ages, feats, stale, cot, ws, wn):
    verts, width = feats.shape
    peers = got.shape[0]
    share = 2 * width // peers
    return call(
        functools.partial(master_kernel, cap),
        "masters",
        (got, adj, ages, feats, stale, cot, ws, wn),
        0,
        [shape((verts, width)), shape((verts, width)), shape((peers, 2 * cap + 2 * share, TILE))],
        (),
        [
            pltpu.VMEM((peers, cap, width), BF),
            pltpu.VMEM((peers, INDEX_ROWS, TILE), BF),
            pltpu.SMEM(ages.shape, jnp.int32),
            like(feats),
            like(stale),
            like(cot),
            like(ws),
            like(wn),
            like(feats),
            like(feats),
            like(feats),
            pltpu.VMEM((peers, 2 * cap, TILE), BF),
            pltpu.VMEM((peers, 2 * share, TILE), BF),
            pltpu.VMEM((verts, width), F32),
            pltpu.SemaphoreType.DMA((9,)),
            pltpu.SemaphoreType.DMA((2 * (verts // ROWS) + 1 + GATHER_STEPS,)),
        ],
    )


def back(cap, got, gp, slot_counts, adj, ws):
    blocks = gp.shape[0] // ROWS
    return call(
        functools.partial(back_kernel, cap),
        "back",
        (got, gp, slot_counts, adj, ws),
        0,
        [shape(gp.shape)],
        (),
        [
            pltpu.VMEM((got.shape[0], 2 * cap, TILE), BF),
            like(gp),
            pltpu.SMEM(slot_counts.shape, jnp.int32),
            like(adj),
            like(ws),
            pltpu.VMEM((got.shape[0] * cap, gp.shape[1]), BF),
            like(gp),
            pltpu.SemaphoreType.DMA((4 + blocks,)),
            pltpu.SemaphoreType.DMA((blocks,)),
        ],
    )[0]


def update(sums, ws, wn):
    return call(update_kernel, "update", (sums, ws, wn), 3, [shape(ws.shape, F32)] * 2, (0, 1), limit=16)


def exchange(x):
    return lax.all_to_all(x, "dom", split_axis=0, concat_axis=0, tiled=True)


def body(
    feats, edge_src, edge_slot, slot_counts, replica_row, stale_agg, bin_ages, cotangent, w_self, w_neigh
):
    verts, width = feats.shape
    peers, cap = replica_row.shape[1:]
    arrived = exchange(scatter(slot_counts, replica_row, edge_src, edge_slot, feats))
    adj = adjacency(edge_src, edge_slot, verts, peers * cap)
    hidden, grad_pre, outgoing = masters(
        cap, arrived, adj, bin_ages, feats, stale_agg, cotangent, w_self, w_neigh
    )
    returned = exchange(outgoing)
    partial = jnp.sum(returned[:, 2 * cap :, :].astype(F32), axis=0)
    groups = lax.axis_size("group")
    step = 1
    while step < groups:
        pairs = [(k, k ^ (2 * step - 1)) for k in range(groups)]
        partial = partial + lax.ppermute(partial, "group", pairs)
        step *= 2
    share = partial.astype(BF)
    sums = exchange(jnp.broadcast_to(share[None], (peers,) + share.shape))
    feat_grad = back(cap, returned, grad_pre, slot_counts, adj, w_self)
    new_self, new_neigh = update(sums, w_self, w_neigh)
    return (hidden, feat_grad, new_self, new_neigh)


def solution(mesh):
    both = ("group", "dom")
    wide = P(both, None)
    placed = (wide, wide, wide, wide, P(both, None, None), wide, P(both), wide, P(), P())
    return jax.shard_map(
        body,
        mesh=mesh,
        in_specs=placed,
        out_specs=(wide, wide, P(), P()),
        check_vma=False,
    )
```

```python
import functools

import jax
import jax.numpy as jnp
from jax import lax
from jax.experimental import pallas as pl
from jax.experimental.pallas import tpu as pltpu
from jax.sharding import PartitionSpec as P

BF = jnp.bfloat16
F8 = jnp.float8_e4m3fn
F32 = jnp.float32
TILE = 128
ROWS = 512
INDEX_ROWS = 16
GATHER_STEPS = 4
NN = (((1,), (0,)), ((), ()))
NT = (((1,), (1,)), ((), ()))
TN = (((0,), (0,)), ((), ()))
MIB = 1024 * 1024


def dot(a, b, dims):
    return lax.dot_general(a, b, dims, preferred_element_type=F32)


def mask(cond):
    return jnp.where(cond, 1.0, 0.0).astype(BF)


def start_all(pairs, sems):
    copies = [pltpu.make_async_copy(src, dst, sems.at[k]) for k, (src, dst) in enumerate(pairs)]
    for copy in copies:
        copy.start()
    return copies


def bin_edges(ref, b, bins, repeats):
    return jnp.concatenate(
        [ref[:, (g * bins + b) * TILE : (g * bins + b + 1) * TILE] for g in range(repeats)], axis=1
    )


def bin_indicators(src_ref, slot_ref, b, bins, repeats, slots):
    src = bin_edges(src_ref, b, bins, repeats) & (TILE - 1)
    slot = bin_edges(slot_ref, b, bins, repeats)
    row = lax.broadcasted_iota(jnp.int32, (TILE, src.shape[1]), 0)
    source = mask(row == src).astype(F8)
    low = mask(row == (slot & (TILE - 1)))
    high = slot >> 7
    return source, [(low * mask(high == h)).astype(F8) for h in range(slots // TILE)]


def scatter_kernel(
    counts_hbm, rows_hbm, src_hbm, slot_hbm, feats_hbm, out_hbm, out_ref, adj_ref, counts_ref, rows_ref, src_ref, slot_ref, feats_ref, sems, out_sems
):
    copies = start_all(
        [
            (src_hbm, src_ref),
            (slot_hbm, slot_ref),
            (feats_hbm, feats_ref),
            (rows_hbm, rows_ref),
            (counts_hbm, counts_ref),
        ],
        sems,
    )
    slots, verts = adj_ref.shape
    peers, cap = rows_ref.shape[1:]
    bins = verts // TILE
    repeats = src_ref.shape[1] // verts
    copies[0].wait()
    copies[1].wait()
    for b in range(bins):
        source, blocks = bin_indicators(src_ref, slot_ref, b, bins, repeats, slots)
        for h, block in enumerate(blocks):
            adj_ref[h * TILE : (h + 1) * TILE, b * TILE : (b + 1) * TILE] = dot(block, source, NT).astype(BF)
    for copy in copies[2:]:
        copy.wait()
    sub = lax.broadcasted_iota(jnp.int32, (INDEX_ROWS, cap), 0)
    slot_in_peer = lax.broadcasted_iota(jnp.int32, (cap, 2 * TILE), 0)
    outs = []
    step = peers // GATHER_STEPS
    for first in range(0, peers, step):
        rows = dot(adj_ref[first * cap : (first + step) * cap, :], feats_ref[...], NN)
        for q in range(first, first + step):
            part = rows[(q - first) * cap : (q - first + 1) * cap, :]
            part = jnp.where(slot_in_peer < counts_ref[0, q], part, 0.0).astype(BF)
            out_ref[q, 0:cap, :] = part[:, :TILE]
            out_ref[q, cap : 2 * cap, :] = part[:, TILE:]
            out_ref[q, 2 * cap :, :] = jnp.zeros((INDEX_ROWS, TILE), BF)
            index = rows_ref[0, q : q + 1, :]
            value = jnp.where(sub == 0, index >> 7, jnp.where(sub == 1, index & (TILE - 1), 0))
            out_ref[q, 2 * cap :, 0:cap] = value.astype(F32).astype(BF)
        those = pl.ds(first, step)
        copy = pltpu.make_async_copy(out_ref.at[those], out_hbm.at[those], out_sems.at[first // step])
        copy.start()
        outs.append(copy)
    for copy in outs:
        copy.wait()


def adjacency_kernel(src_hbm, slot_hbm, out_hbm, src_ref, slot_ref, adj_ref, sems, out_sems):
    copies = start_all([(src_hbm, src_ref), (slot_hbm, slot_ref)], sems)
    verts, slots = adj_ref.shape
    bins = verts // TILE
    repeats = src_ref.shape[1] // verts
    for copy in copies:
        copy.wait()
    outs = []
    per = ROWS // TILE
    for b in range(bins):
        source, blocks = bin_indicators(src_ref, slot_ref, b, bins, repeats, slots)
        for h, block in enumerate(blocks):
            adj_ref[b * TILE : (b + 1) * TILE, h * TILE : (h + 1) * TILE] = dot(source, block, NT).astype(BF)
        if b % per == per - 1:
            rows = pl.ds((b // per) * ROWS, ROWS)
            copy = pltpu.make_async_copy(adj_ref.at[rows], out_hbm.at[rows], out_sems.at[b // per])
            copy.start()
            outs.append(copy)
    for copy in outs:
        copy.wait()


def master_kernel(
    cap,
    got_hbm,
    adj_hbm,
    ages_hbm,
    feats_hbm,
    stale_hbm,
    cot_hbm,
    ws_hbm,
    wn_hbm,
    hidden_hbm,
    gp_hbm,
    out_hbm,
    arr_ref,
    coded_ref,
    ages_ref,
    feats_ref,
    stale_ref,
    cot_ref,
    ws_ref,
    wn_ref,
    hidden_ref,
    gp_ref,
    ga_ref,
    back_ref,
    share_ref,
    agg_ref,
    sems,
    out_sems,
):
    peers = arr_ref.shape[0]
    verts, width = feats_ref.shape
    slots = peers * cap
    blocks = verts // ROWS
    copies = start_all(
        [
            (got_hbm.at[:, pl.ds(2 * cap, INDEX_ROWS), :], coded_ref),
            (got_hbm.at[:, pl.ds(0, cap), :], arr_ref.at[:, :, pl.ds(0, TILE)]),
            (got_hbm.at[:, pl.ds(cap, cap), :], arr_ref.at[:, :, pl.ds(TILE, TILE)]),
            (ages_hbm, ages_ref),
            (stale_hbm, stale_ref),
            (feats_hbm, feats_ref),
            (ws_hbm, ws_ref),
            (wn_hbm, wn_ref),
            (cot_hbm, cot_ref),
        ],
        sems,
    )
    copies[0].wait()
    coded = coded_ref[...].reshape(peers * INDEX_ROWS, TILE)
    pick_row = lax.broadcasted_iota(jnp.int32, (peers, peers * INDEX_ROWS), 1)
    pick_peer = lax.broadcasted_iota(jnp.int32, (peers, peers * INDEX_ROWS), 0) * INDEX_ROWS
    high = dot(mask(pick_row == pick_peer), coded, NN).astype(BF)
    low = dot(mask(pick_row == pick_peer + 1), coded, NN).astype(BF)
    place = lax.broadcasted_iota(jnp.int32, (peers, cap, TILE), 1).reshape(slots, TILE)
    peer = lax.broadcasted_iota(jnp.int32, (peers, cap, TILE), 0).reshape(slots, TILE)
    lane = lax.broadcasted_iota(jnp.int32, (slots, TILE), 1)
    at_place = place == lane
    spread = mask(at_place)
    value = dot(high, spread, NT) * float(TILE) + dot(low, spread, NT)
    slot = lax.broadcasted_iota(jnp.int32, (peers, slots), 1)
    least = lax.broadcasted_iota(jnp.int32, (peers, slots), 0) * cap
    own = (slot >= least) & (slot < least + cap)
    row_index = jnp.sum(jnp.where(own, value, 0.0), axis=0, keepdims=True).astype(jnp.int32)
    sub = lax.broadcasted_iota(jnp.int32, (TILE, slots), 0)
    low_hot = mask(sub == (row_index & (TILE - 1)))
    row_high = row_index >> 7
    at_peer = mask(peer == lane)[:, :peers]
    value_c = dot(at_peer, high, NN) * float(TILE) + dot(at_peer, low, NN)
    col_index = jnp.sum(jnp.where(at_place, value_c, 0.0), axis=1, keepdims=True).astype(jnp.int32)
    for copy in copies[1:3]:
        copy.wait()
    total = None
    outs = []
    per = ROWS // TILE

    def send(src, dst):
        copy = pltpu.make_async_copy(src, dst, out_sems.at[len(outs)])
        copy.start()
        outs.append(copy)

    for block in range(blocks):
        hot = jnp.concatenate([low_hot * mask(row_high == block * per + k) for k in range(per)], axis=0)
        agg_ref[block * ROWS : (block + 1) * ROWS, :] = dot(hot, arr_ref[...].reshape(slots, width), NN)
    for block in range(blocks):
        rows = slice(block * ROWS, (block + 1) * ROWS)
        agg = agg_ref[rows, :]
        if block == 0:
            copies[3].wait()
            copies[4].wait()
        aged = []
        for k in range(block * per, (block + 1) * per):
            age = jnp.full((1, width), ages_ref[k], jnp.int32).astype(F32)
            aged.append(stale_ref[k * TILE : (k + 1) * TILE, :].astype(F32) * (1.0 / (1.0 + age)))
        agg = agg + jnp.concatenate(aged, axis=0)
        inverse = lax.rsqrt(jnp.mean(agg * agg, axis=1, keepdims=True) + 1e-05)
        normed = (agg * inverse).astype(BF)
        if block == 0:
            for copy in copies[5:]:
                copy.wait()
        feats = feats_ref[rows, :]
        pre = dot(feats, ws_ref[...], NN) + dot(normed, wn_ref[...], NN)
        sig = jax.nn.sigmoid(pre)
        hidden_ref[rows, :] = (pre * sig).astype(BF)
        gp = (cot_ref[rows, :].astype(F32) * sig * (1.0 + pre * (1.0 - sig))).astype(BF)
        gp_ref[rows, :] = gp
        part = pl.ds(block * ROWS, ROWS)
        send(hidden_ref.at[part], hidden_hbm.at[part])
        send(gp_ref.at[part], gp_hbm.at[part])
        grads = jnp.concatenate([dot(feats, gp, TN), dot(normed, gp, TN)], axis=0)
        total = grads if total is None else total + grads
        gn = dot(gp, wn_ref[...], NT)
        inner = jnp.mean(gn * agg, axis=1, keepdims=True)
        ga_ref[rows, :] = (inverse * (gn - agg * (inverse * inverse * inner))).astype(BF)
    total = total.astype(BF)
    share = 2 * width // peers
    share_ref[:, :share, :] = total[:, :TILE].reshape(peers, share, TILE)
    share_ref[:, share:, :] = total[:, TILE:].reshape(peers, share, TILE)
    send(share_ref, out_hbm.at[:, pl.ds(2 * cap, 2 * share), :])
    step = peers // GATHER_STEPS
    for first in range(0, peers, step):
        part = slice(first * cap, (first + step) * cap)
        lanes = lax.broadcasted_iota(jnp.int32, (step * cap, verts), 1)
        rows = dot(mask(lanes == col_index[part, :]), ga_ref[...], NN).astype(BF)
        back_ref[first : first + step, 0:cap, :] = rows[:, :TILE].reshape(step, cap, TILE)
        back_ref[first : first + step, cap:, :] = rows[:, TILE:].reshape(step, cap, TILE)
        those = pl.ds(first, step)
        send(back_ref.at[those], out_hbm.at[those, pl.ds(0, 2 * cap), :])
    for copy in outs:
        copy.wait()


def back_kernel(
    cap, got_hbm, gp_hbm, counts_hbm, adj_hbm, ws_hbm, out_hbm, got_ref, gp_ref, counts_ref, adj_ref, ws_ref, grad_ref, out_ref, sems, out_sems
):
    verts = out_ref.shape[0]
    blocks = verts // ROWS
    pairs = [
        (counts_hbm, counts_ref),
        (got_hbm.at[:, pl.ds(0, 2 * cap), :], got_ref),
        (ws_hbm, ws_ref),
        (gp_hbm, gp_ref),
    ]
    for block in range(blocks):
        part = pl.ds(block * ROWS, ROWS)
        pairs.append((adj_hbm.at[part], adj_ref.at[part]))
    copies = start_all(pairs, sems)
    peers = got_ref.shape[0]
    copies[0].wait()
    copies[1].wait()
    slot_in_peer = lax.broadcasted_iota(jnp.int32, (cap, TILE), 0)
    for q in range(peers):
        live = slot_in_peer < counts_ref[0, q]
        for half in range(2):
            rows = got_ref[q, half * cap : (half + 1) * cap, :]
            grad_ref[q * cap : (q + 1) * cap, half * TILE : (half + 1) * TILE] = jnp.where(
                live, rows.astype(F32), 0.0
            ).astype(BF)
    outs = []
    copies[2].wait()
    copies[3].wait()
    for block in range(blocks):
        rows = slice(block * ROWS, (block + 1) * ROWS)
        own = dot(gp_ref[rows, :], ws_ref[...], NT)
        copies[4 + block].wait()
        out_ref[rows, :] = (dot(adj_ref[rows, :], grad_ref[...], NN) + own).astype(BF)
        part = pl.ds(block * ROWS, ROWS)
        copy = pltpu.make_async_copy(out_ref.at[part], out_hbm.at[part], out_sems.at[block])
        copy.start()
        outs.append(copy)
    for copy in outs:
        copy.wait()


def update_kernel(sum_ref, ws_ref, wn_ref, new_s_ref, new_n_ref):
    peers, share = sum_ref.shape[0], sum_ref.shape[1] // 2
    left = sum_ref[:, :share, :].astype(F32).reshape(peers * share, TILE)
    right = sum_ref[:, share:, :].astype(F32).reshape(peers * share, TILE)
    total = jnp.concatenate([left, right], axis=1)
    norm = jnp.sqrt(jnp.sum(total * total, keepdims=True))
    scale = 8.0 * jnp.minimum(1.0, 1.0 / norm)
    half = new_s_ref.shape[0]
    new_s_ref[...] = ws_ref[...].astype(F32) - scale * total[:half]
    new_n_ref[...] = wn_ref[...].astype(F32) - scale * total[half:]


HBM = pl.BlockSpec(memory_space=pltpu.HBM)
VMEM = pl.BlockSpec(memory_space=pltpu.VMEM)


def call(kernel, name, args, near, outs, out_near, scratch=(), flops=10**9, limit=56):
    size = sum(a.size * a.dtype.itemsize for a in args)
    return pl.pallas_call(
        kernel,
        name=name,
        in_specs=[VMEM if k < near else HBM for k in range(len(args))],
        out_specs=[VMEM if k in out_near else HBM for k in range(len(outs))],
        out_shape=outs,
        scratch_shapes=list(scratch),
        compiler_params=pltpu.CompilerParams(vmem_limit_bytes=limit * MIB),
        cost_estimate=pl.CostEstimate(flops=flops, bytes_accessed=size, transcendentals=0),
    )(*args)


def shape(dims, dtype=BF):
    return jax.ShapeDtypeStruct(dims, dtype)


def like(x):
    return pltpu.VMEM(x.shape, x.dtype)


def scatter(slot_counts, replica_row, edge_src, edge_slot, feats):
    peers, cap = replica_row.shape[1:]
    return call(
        scatter_kernel,
        "scatter",
        (slot_counts, replica_row, edge_src, edge_slot, feats),
        0,
        [shape((peers, 2 * cap + INDEX_ROWS, TILE))],
        (),
        [
            pltpu.VMEM((peers, 2 * cap + INDEX_ROWS, TILE), BF),
            pltpu.VMEM((peers * cap, feats.shape[0]), BF),
            pltpu.SMEM(slot_counts.shape, jnp.int32),
            like(replica_row),
            like(edge_src),
            like(edge_slot),
            like(feats),
            pltpu.SemaphoreType.DMA((5,)),
            pltpu.SemaphoreType.DMA((GATHER_STEPS,)),
        ],
    )[0]


def adjacency(edge_src, edge_slot, verts, slots):
    return call(
        adjacency_kernel,
        "adjacency",
        (edge_src, edge_slot),
        0,
        [shape((verts, slots))],
        (),
        [
            like(edge_src),
            like(edge_slot),
            pltpu.VMEM((verts, slots), BF),
            pltpu.SemaphoreType.DMA((2,)),
            pltpu.SemaphoreType.DMA((verts // ROWS,)),
        ],
        flops=6 * 10**9,
    )[0]


def masters(cap, got, adj, ages, feats, stale, cot, ws, wn):
    verts, width = feats.shape
    peers = got.shape[0]
    share = 2 * width // peers
    return call(
        functools.partial(master_kernel, cap),
        "masters",
        (got, adj, ages, feats, stale, cot, ws, wn),
        0,
        [shape((verts, width)), shape((verts, width)), shape((peers, 2 * cap + 2 * share, TILE))],
        (),
        [
            pltpu.VMEM((peers, cap, width), BF),
            pltpu.VMEM((peers, INDEX_ROWS, TILE), BF),
            pltpu.SMEM(ages.shape, jnp.int32),
            like(feats),
            like(stale),
            like(cot),
            like(ws),
            like(wn),
            like(feats),
            like(feats),
            like(feats),
            pltpu.VMEM((peers, 2 * cap, TILE), BF),
            pltpu.VMEM((peers, 2 * share, TILE), BF),
            pltpu.VMEM((verts, width), F32),
            pltpu.SemaphoreType.DMA((9,)),
            pltpu.SemaphoreType.DMA((2 * (verts // ROWS) + 1 + GATHER_STEPS,)),
        ],
        limit=50,
    )


def back(cap, got, gp, slot_counts, adj, ws):
    blocks = gp.shape[0] // ROWS
    return call(
        functools.partial(back_kernel, cap),
        "back",
        (got, gp, slot_counts, adj, ws),
        0,
        [shape(gp.shape)],
        (),
        [
            pltpu.VMEM((got.shape[0], 2 * cap, TILE), BF),
            like(gp),
            pltpu.SMEM(slot_counts.shape, jnp.int32),
            like(adj),
            like(ws),
            pltpu.VMEM((got.shape[0] * cap, gp.shape[1]), BF),
            like(gp),
            pltpu.SemaphoreType.DMA((4 + blocks,)),
            pltpu.SemaphoreType.DMA((blocks,)),
        ],
        limit=50,
    )[0]


def update(sums, ws, wn):
    return call(update_kernel, "update", (sums, ws, wn), 3, [shape(ws.shape, F32)] * 2, (0, 1), limit=16)


def exchange(x):
    return lax.all_to_all(x, "dom", split_axis=0, concat_axis=0, tiled=True)


def body(
    feats, edge_src, edge_slot, slot_counts, replica_row, stale_agg, bin_ages, cotangent, w_self, w_neigh
):
    verts, width = feats.shape
    peers, cap = replica_row.shape[1:]
    arrived = exchange(scatter(slot_counts, replica_row, edge_src, edge_slot, feats))
    adj = adjacency(edge_src, edge_slot, verts, peers * cap)
    hidden, grad_pre, outgoing = masters(
        cap, arrived, adj, bin_ages, feats, stale_agg, cotangent, w_self, w_neigh
    )
    returned = exchange(outgoing)
    partial = jnp.sum(returned[:, 2 * cap :, :].astype(F32), axis=0)
    groups = range(lax.axis_size("group"))
    near, far, across = (
        lax.ppermute(partial, "group", [(k, k ^ other) for k in groups]) for other in (1, 2, 3)
    )
    share = ((partial + near) + (far + across)).astype(BF)
    sums = exchange(jnp.broadcast_to(share[None], (peers,) + share.shape))
    feat_grad = back(cap, returned, grad_pre, slot_counts, adj, w_self)
    new_self, new_neigh = update(sums, w_self, w_neigh)
    return (hidden, feat_grad, new_self, new_neigh)


def solution(mesh):
    both = ("group", "dom")
    wide = P(both, None)
    placed = (wide, wide, wide, wide, P(both, None, None), wide, P(both), wide, P(), P())
    return jax.shard_map(
        body,
        mesh=mesh,
        in_specs=placed,
        out_specs=(wide, wide, P(), P()),
        check_vma=False,
    )
```

```python
import functools

import jax
import jax.numpy as jnp
from jax import lax
from jax.experimental import pallas as pl
from jax.experimental.pallas import tpu as pltpu
from jax.sharding import PartitionSpec as P

BF = jnp.bfloat16
F8 = jnp.float8_e4m3fn
F32 = jnp.float32
TILE = 128
ROWS = 512
INDEX_ROWS = 16
GATHER_STEPS = 4
NN = (((1,), (0,)), ((), ()))
NT = (((1,), (1,)), ((), ()))
TN = (((0,), (0,)), ((), ()))
MIB = 1024 * 1024


def dot(a, b, dims):
    return lax.dot_general(a, b, dims, preferred_element_type=F32)


def mask(cond):
    return jnp.where(cond, 1.0, 0.0).astype(BF)


def start_all(pairs, sems):
    copies = [pltpu.make_async_copy(src, dst, sems.at[k]) for k, (src, dst) in enumerate(pairs)]
    for copy in copies:
        copy.start()
    return copies


def bin_edges(ref, b, bins, repeats):
    return jnp.concatenate(
        [ref[:, (g * bins + b) * TILE : (g * bins + b + 1) * TILE] for g in range(repeats)], axis=1
    )


def bin_indicators(src_ref, slot_ref, b, bins, repeats, slots):
    src = bin_edges(src_ref, b, bins, repeats) & (TILE - 1)
    slot = bin_edges(slot_ref, b, bins, repeats)
    row = lax.broadcasted_iota(jnp.int32, (TILE, src.shape[1]), 0)
    source = mask(row == src).astype(F8)
    low = mask(row == (slot & (TILE - 1)))
    high = slot >> 7
    return source, [(low * mask(high == h)).astype(F8) for h in range(slots // TILE)]


def scatter_kernel(
    counts_hbm, rows_hbm, src_hbm, slot_hbm, feats_hbm, out_hbm, out_ref, adj_ref, counts_ref, rows_ref, src_ref, slot_ref, feats_ref, sems, out_sems
):
    copies = start_all(
        [
            (src_hbm, src_ref),
            (slot_hbm, slot_ref),
            (feats_hbm, feats_ref),
            (rows_hbm, rows_ref),
            (counts_hbm, counts_ref),
        ],
        sems,
    )
    slots, verts = adj_ref.shape
    peers, cap = rows_ref.shape[1:]
    bins = verts // TILE
    repeats = src_ref.shape[1] // verts
    copies[0].wait()
    copies[1].wait()
    for b in range(bins):
        source, blocks = bin_indicators(src_ref, slot_ref, b, bins, repeats, slots)
        for h, block in enumerate(blocks):
            adj_ref[h * TILE : (h + 1) * TILE, b * TILE : (b + 1) * TILE] = dot(block, source, NT).astype(BF)
    for copy in copies[2:]:
        copy.wait()
    sub = lax.broadcasted_iota(jnp.int32, (INDEX_ROWS, cap), 0)
    slot_in_peer = lax.broadcasted_iota(jnp.int32, (cap, 2 * TILE), 0)
    outs = []
    step = peers // GATHER_STEPS
    for first in range(0, peers, step):
        rows = dot(adj_ref[first * cap : (first + step) * cap, :], feats_ref[...], NN)
        for q in range(first, first + step):
            part = rows[(q - first) * cap : (q - first + 1) * cap, :]
            part = jnp.where(slot_in_peer < counts_ref[0, q], part, 0.0).astype(BF)
            out_ref[q, 0:cap, :] = part[:, :TILE]
            out_ref[q, cap : 2 * cap, :] = part[:, TILE:]
            out_ref[q, 2 * cap :, :] = jnp.zeros((INDEX_ROWS, TILE), BF)
            index = rows_ref[0, q : q + 1, :]
            value = jnp.where(sub == 0, index >> 7, jnp.where(sub == 1, index & (TILE - 1), 0))
            out_ref[q, 2 * cap :, 0:cap] = value.astype(F32).astype(BF)
        those = pl.ds(first, step)
        copy = pltpu.make_async_copy(out_ref.at[those], out_hbm.at[those], out_sems.at[first // step])
        copy.start()
        outs.append(copy)
    for copy in outs:
        copy.wait()


def adjacency_kernel(src_hbm, slot_hbm, out_hbm, src_ref, slot_ref, adj_ref, sems, out_sems):
    copies = start_all([(src_hbm, src_ref), (slot_hbm, slot_ref)], sems)
    verts, slots = adj_ref.shape
    bins = verts // TILE
    repeats = src_ref.shape[1] // verts
    for copy in copies:
        copy.wait()
    outs = []
    per = ROWS // TILE
    for b in range(bins):
        source, blocks = bin_indicators(src_ref, slot_ref, b, bins, repeats, slots)
        for h, block in enumerate(blocks):
            adj_ref[b * TILE : (b + 1) * TILE, h * TILE : (h + 1) * TILE] = dot(source, block, NT).astype(BF)
        if b % per == per - 1:
            rows = pl.ds((b // per) * ROWS, ROWS)
            copy = pltpu.make_async_copy(adj_ref.at[rows], out_hbm.at[rows], out_sems.at[b // per])
            copy.start()
            outs.append(copy)
    for copy in outs:
        copy.wait()


def index_digits(cap, got_ref):
    peers = got_ref.shape[0]
    coded = got_ref[:, 2 * cap :, :].reshape(peers * INDEX_ROWS, TILE)
    pick_row = lax.broadcasted_iota(jnp.int32, (peers, peers * INDEX_ROWS), 1)
    pick_peer = lax.broadcasted_iota(jnp.int32, (peers, peers * INDEX_ROWS), 0) * INDEX_ROWS
    high = dot(mask(pick_row == pick_peer), coded, NN).astype(BF)
    low = dot(mask(pick_row == pick_peer + 1), coded, NN).astype(BF)
    return high, low


def master_kernel(
    cap,
    got_ref,
    ws_ref,
    wn_ref,
    adj_hbm,
    ages_hbm,
    feats_hbm,
    stale_hbm,
    cot_hbm,
    hidden_hbm,
    gp_hbm,
    agg_hbm,
    share_ref,
    arr_ref,
    ages_ref,
    feats_ref,
    stale_ref,
    cot_ref,
    hidden_ref,
    gp_ref,
    agg_ref,
    sems,
    out_sems,
):
    peers = got_ref.shape[0]
    verts, width = feats_ref.shape
    slots = peers * cap
    blocks = verts // ROWS
    copies = start_all(
        [(ages_hbm, ages_ref), (stale_hbm, stale_ref), (feats_hbm, feats_ref), (cot_hbm, cot_ref)], sems
    )
    high, low = index_digits(cap, got_ref)
    place = lax.broadcasted_iota(jnp.int32, (peers, cap, TILE), 1).reshape(slots, TILE)
    spread = mask(place == lax.broadcasted_iota(jnp.int32, (slots, TILE), 1))
    value = dot(high, spread, NT) * float(TILE) + dot(low, spread, NT)
    slot = lax.broadcasted_iota(jnp.int32, (peers, slots), 1)
    least = lax.broadcasted_iota(jnp.int32, (peers, slots), 0) * cap
    own = (slot >= least) & (slot < least + cap)
    row_index = jnp.sum(jnp.where(own, value, 0.0), axis=0, keepdims=True).astype(jnp.int32)
    sub = lax.broadcasted_iota(jnp.int32, (TILE, slots), 0)
    low_hot = mask(sub == (row_index & (TILE - 1)))
    row_high = row_index >> 7
    arr_ref[:, :TILE] = got_ref[:, 0:cap, :].reshape(slots, TILE)
    arr_ref[:, TILE:] = got_ref[:, cap : 2 * cap, :].reshape(slots, TILE)
    per = ROWS // TILE
    for block in range(blocks):
        hot = jnp.concatenate([low_hot * mask(row_high == block * per + k) for k in range(per)], axis=0)
        agg_ref[block * ROWS : (block + 1) * ROWS, :] = dot(hot, arr_ref[...], NN)
    for copy in copies:
        copy.wait()
    total = None
    outs = []
    for block in range(blocks):
        rows = slice(block * ROWS, (block + 1) * ROWS)
        aged = []
        for k in range(block * per, (block + 1) * per):
            age = jnp.full((1, width), ages_ref[k], jnp.int32).astype(F32)
            aged.append(stale_ref[k * TILE : (k + 1) * TILE, :].astype(F32) * (1.0 / (1.0 + age)))
        agg = agg_ref[rows, :] + jnp.concatenate(aged, axis=0)
        agg_ref[rows, :] = agg
        inverse = lax.rsqrt(jnp.mean(agg * agg, axis=1, keepdims=True) + 1e-05)
        normed = (agg * inverse).astype(BF)
        feats = feats_ref[rows, :]
        pre = dot(feats, ws_ref[...], NN) + dot(normed, wn_ref[...], NN)
        sig = jax.nn.sigmoid(pre)
        hidden_ref[rows, :] = (pre * sig).astype(BF)
        gp = (cot_ref[rows, :].astype(F32) * sig * (1.0 + pre * (1.0 - sig))).astype(BF)
        gp_ref[rows, :] = gp
        part = pl.ds(block * ROWS, ROWS)
        for near, far in ((agg_ref, agg_hbm), (gp_ref, gp_hbm), (hidden_ref, hidden_hbm)):
            copy = pltpu.make_async_copy(near.at[part], far.at[part], out_sems.at[len(outs)])
            copy.start()
            outs.append(copy)
        grads = jnp.concatenate([dot(feats, gp, TN), dot(normed, gp, TN)], axis=0)
        total = grads if total is None else total + grads
    total = total.astype(BF)
    share = 2 * width // peers
    share_ref[:, :share, :] = total[:, :TILE].reshape(peers, share, TILE)
    share_ref[:, share:, :] = total[:, TILE:].reshape(peers, share, TILE)
    for copy in outs:
        copy.wait()


def outgoing_kernel(cap, got_ref, wn_ref, gp_hbm, agg_hbm, out_ref, gp_ref, agg_ref, ga_ref, sems):
    peers = got_ref.shape[0]
    verts = gp_ref.shape[0]
    slots = peers * cap
    parts = [pl.ds(block * ROWS, ROWS) for block in range(verts // ROWS)]
    copies = start_all(
        [(far.at[part], near.at[part]) for part in parts for far, near in ((gp_hbm, gp_ref), (agg_hbm, agg_ref))],
        sems,
    )
    for block in range(verts // ROWS):
        rows = slice(block * ROWS, (block + 1) * ROWS)
        copies[2 * block].wait()
        copies[2 * block + 1].wait()
        agg = agg_ref[rows, :]
        inverse = lax.rsqrt(jnp.mean(agg * agg, axis=1, keepdims=True) + 1e-05)
        gn = dot(gp_ref[rows, :], wn_ref[...], NT)
        inner = jnp.mean(gn * agg, axis=1, keepdims=True)
        ga_ref[rows, :] = (inverse * (gn - agg * (inverse * inverse * inner))).astype(BF)
    high, low = index_digits(cap, got_ref)
    place = lax.broadcasted_iota(jnp.int32, (peers, cap, TILE), 1).reshape(slots, TILE)
    peer = lax.broadcasted_iota(jnp.int32, (peers, cap, TILE), 0).reshape(slots, TILE)
    lane = lax.broadcasted_iota(jnp.int32, (slots, TILE), 1)
    at_peer = mask(peer == lane)[:, :peers]
    value = dot(at_peer, high, NN) * float(TILE) + dot(at_peer, low, NN)
    index = jnp.sum(jnp.where(place == lane, value, 0.0), axis=1, keepdims=True).astype(jnp.int32)
    step = peers // GATHER_STEPS
    for first in range(0, peers, step):
        part = slice(first * cap, (first + step) * cap)
        lanes = lax.broadcasted_iota(jnp.int32, (step * cap, verts), 1)
        rows = dot(mask(lanes == index[part, :]), ga_ref[...], NN).astype(BF)
        out_ref[first : first + step, 0:cap, :] = rows[:, :TILE].reshape(step, cap, TILE)
        out_ref[first : first + step, cap:, :] = rows[:, TILE:].reshape(step, cap, TILE)


def sum_kernel(parts_ref, after_hbm, out_ref):
    out_ref[...] = jnp.sum(parts_ref[...].astype(F32), axis=0)


def share_kernel(own_ref, near_ref, far_ref, across_ref, after_hbm, out_ref):
    total = (own_ref[...] + near_ref[...]) + (far_ref[...] + across_ref[...])
    out_ref[...] = jnp.broadcast_to(total.astype(BF)[None], out_ref.shape)


def back_kernel(
    cap, got_hbm, gp_hbm, counts_hbm, adj_hbm, ws_hbm, out_hbm, got_ref, gp_ref, counts_ref, adj_ref, ws_ref, grad_ref, out_ref, sems, out_sems
):
    verts = out_ref.shape[0]
    blocks = verts // ROWS
    pairs = [
        (counts_hbm, counts_ref),
        (got_hbm, got_ref),
        (ws_hbm, ws_ref),
        (gp_hbm, gp_ref),
    ]
    for block in range(blocks):
        part = pl.ds(block * ROWS, ROWS)
        pairs.append((adj_hbm.at[part], adj_ref.at[part]))
    copies = start_all(pairs, sems)
    peers = got_ref.shape[0]
    copies[0].wait()
    copies[1].wait()
    slot_in_peer = lax.broadcasted_iota(jnp.int32, (cap, TILE), 0)
    for q in range(peers):
        live = slot_in_peer < counts_ref[0, q]
        for half in range(2):
            rows = got_ref[q, half * cap : (half + 1) * cap, :]
            grad_ref[q * cap : (q + 1) * cap, half * TILE : (half + 1) * TILE] = jnp.where(
                live, rows.astype(F32), 0.0
            ).astype(BF)
    outs = []
    copies[2].wait()
    copies[3].wait()
    for block in range(blocks):
        rows = slice(block * ROWS, (block + 1) * ROWS)
        own = dot(gp_ref[rows, :], ws_ref[...], NT)
        copies[4 + block].wait()
        out_ref[rows, :] = (dot(adj_ref[rows, :], grad_ref[...], NN) + own).astype(BF)
        part = pl.ds(block * ROWS, ROWS)
        copy = pltpu.make_async_copy(out_ref.at[part], out_hbm.at[part], out_sems.at[block])
        copy.start()
        outs.append(copy)
    for copy in outs:
        copy.wait()


def update_kernel(sum_ref, ws_ref, wn_ref, new_s_ref, new_n_ref):
    peers, share = sum_ref.shape[0], sum_ref.shape[1] // 2
    left = sum_ref[:, :share, :].astype(F32).reshape(peers * share, TILE)
    right = sum_ref[:, share:, :].astype(F32).reshape(peers * share, TILE)
    total = jnp.concatenate([left, right], axis=1)
    norm = jnp.sqrt(jnp.sum(total * total, keepdims=True))
    scale = 8.0 * jnp.minimum(1.0, 1.0 / norm)
    half = new_s_ref.shape[0]
    new_s_ref[...] = ws_ref[...].astype(F32) - scale * total[:half]
    new_n_ref[...] = wn_ref[...].astype(F32) - scale * total[half:]


HBM = pl.BlockSpec(memory_space=pltpu.HBM)
VMEM = pl.BlockSpec(memory_space=pltpu.VMEM)


def call(kernel, name, args, near, outs, out_near, scratch=(), flops=10**9, limit=56):
    size = sum(a.size * a.dtype.itemsize for a in args)
    return pl.pallas_call(
        kernel,
        name=name,
        in_specs=[VMEM if k < near else HBM for k in range(len(args))],
        out_specs=[VMEM if k in out_near else HBM for k in range(len(outs))],
        out_shape=outs,
        scratch_shapes=list(scratch),
        compiler_params=pltpu.CompilerParams(vmem_limit_bytes=limit * MIB),
        cost_estimate=pl.CostEstimate(flops=flops, bytes_accessed=size, transcendentals=0),
    )(*args)


def shape(dims, dtype=BF):
    return jax.ShapeDtypeStruct(dims, dtype)


def like(x):
    return pltpu.VMEM(x.shape, x.dtype)


def scatter(slot_counts, replica_row, edge_src, edge_slot, feats):
    peers, cap = replica_row.shape[1:]
    return call(
        scatter_kernel,
        "scatter",
        (slot_counts, replica_row, edge_src, edge_slot, feats),
        0,
        [shape((peers, 2 * cap + INDEX_ROWS, TILE))],
        (),
        [
            pltpu.VMEM((peers, 2 * cap + INDEX_ROWS, TILE), BF),
            pltpu.VMEM((peers * cap, feats.shape[0]), BF),
            pltpu.SMEM(slot_counts.shape, jnp.int32),
            like(replica_row),
            like(edge_src),
            like(edge_slot),
            like(feats),
            pltpu.SemaphoreType.DMA((5,)),
            pltpu.SemaphoreType.DMA((GATHER_STEPS,)),
        ],
    )[0]


def adjacency(edge_src, edge_slot, verts, slots):
    return call(
        adjacency_kernel,
        "adjacency",
        (edge_src, edge_slot),
        0,
        [shape((verts, slots))],
        (),
        [
            like(edge_src),
            like(edge_slot),
            pltpu.VMEM((verts, slots), BF),
            pltpu.SemaphoreType.DMA((2,)),
            pltpu.SemaphoreType.DMA((verts // ROWS,)),
        ],
        flops=6 * 10**9,
    )[0]


def masters(cap, got, adj, ages, feats, stale, cot, ws, wn):
    verts, width = feats.shape
    peers = got.shape[0]
    share = 2 * width // peers
    return call(
        functools.partial(master_kernel, cap),
        "masters",
        (got, ws, wn, adj, ages, feats, stale, cot),
        3,
        [
            shape((verts, width)),
            shape((verts, width)),
            shape((verts, width), F32),
            shape((peers, 2 * share, TILE)),
        ],
        (3,),
        [
            pltpu.VMEM((peers * cap, width), BF),
            pltpu.SMEM(ages.shape, jnp.int32),
            like(feats),
            like(stale),
            like(cot),
            like(feats),
            like(feats),
            pltpu.VMEM((verts, width), F32),
            pltpu.SemaphoreType.DMA((4,)),
            pltpu.SemaphoreType.DMA((3 * (verts // ROWS),)),
        ],
        limit=52,
    )


def outgoing(cap, got, gp, agg, wn):
    return call(
        functools.partial(outgoing_kernel, cap),
        "outgoing",
        (got, wn, gp, agg),
        2,
        [shape((got.shape[0], 2 * cap, TILE))],
        (0,),
        [like(gp), like(agg), like(gp), pltpu.SemaphoreType.DMA((2 * (gp.shape[0] // ROWS),))],
        limit=52,
    )[0]


def summed(parts, after):
    return call(sum_kernel, "summed", (parts, after), 1, [shape(parts.shape[1:], F32)], (0,), flops=10**6, limit=16)[0]


def shares(parts, after):
    peers = after.shape[0]
    return call(
        share_kernel, "shares", (*parts, after), 4, [shape((peers,) + parts[0].shape)], (0,), flops=10**6, limit=16
    )[0]


def back(cap, got, gp, slot_counts, adj, ws):
    blocks = gp.shape[0] // ROWS
    return call(
        functools.partial(back_kernel, cap),
        "back",
        (got, gp, slot_counts, adj, ws),
        0,
        [shape(gp.shape)],
        (),
        [
            pltpu.VMEM((got.shape[0], 2 * cap, TILE), BF),
            like(gp),
            pltpu.SMEM(slot_counts.shape, jnp.int32),
            like(adj),
            like(ws),
            pltpu.VMEM((got.shape[0] * cap, gp.shape[1]), BF),
            like(gp),
            pltpu.SemaphoreType.DMA((4 + blocks,)),
            pltpu.SemaphoreType.DMA((blocks,)),
        ],
        limit=50,
    )[0]


def update(sums, ws, wn):
    return call(update_kernel, "update", (sums, ws, wn), 3, [shape(ws.shape, F32)] * 2, (0, 1), limit=16)


def exchange(x):
    return lax.all_to_all(x, "dom", split_axis=0, concat_axis=0, tiled=True)


def body(
    feats, edge_src, edge_slot, slot_counts, replica_row, stale_agg, bin_ages, cotangent, w_self, w_neigh
):
    verts, width = feats.shape
    peers, cap = replica_row.shape[1:]
    arrived = exchange(scatter(slot_counts, replica_row, edge_src, edge_slot, feats))
    adj = adjacency(edge_src, edge_slot, verts, peers * cap)
    hidden, grad_pre, aggregate, parts = masters(
        cap, arrived, adj, bin_ages, feats, stale_agg, cotangent, w_self, w_neigh
    )
    parts = exchange(parts)
    sent = outgoing(cap, arrived, grad_pre, aggregate, w_neigh)
    own = summed(parts, sent)
    groups = range(lax.axis_size("group"))
    others = [lax.ppermute(own, "group", [(k, k ^ other) for k in groups]) for other in (1, 2, 3)]
    returned = exchange(sent)
    sums = exchange(shares((own, *others), returned))
    feat_grad = back(cap, returned, grad_pre, slot_counts, adj, w_self)
    new_self, new_neigh = update(sums, w_self, w_neigh)
    return (hidden, feat_grad, new_self, new_neigh)


def solution(mesh):
    both = ("group", "dom")
    wide = P(both, None)
    placed = (wide, wide, wide, wide, P(both, None, None), wide, P(both), wide, P(), P())
    return jax.shard_map(
        body,
        mesh=mesh,
        in_specs=placed,
        out_specs=(wide, wide, P(), P()),
        check_vma=False,
    )
```

```python
import functools

import jax
import jax.numpy as jnp
from jax import lax
from jax.experimental import pallas as pl
from jax.experimental.pallas import tpu as pltpu
from jax.sharding import PartitionSpec as P

BF = jnp.bfloat16
F8 = jnp.float8_e4m3fn
F32 = jnp.float32
TILE = 128
ROWS = 512
FINE = 256
INDEX_ROWS = 8
GATHER_STEPS = 4
NN = (((1,), (0,)), ((), ()))
NT = (((1,), (1,)), ((), ()))
TN = (((0,), (0,)), ((), ()))
MIB = 1024 * 1024


def dot(a, b, dims):
    return lax.dot_general(a, b, dims, preferred_element_type=F32)


def mask(cond):
    return jnp.where(cond, 1.0, 0.0).astype(BF)


def start_all(pairs, sems):
    copies = [pltpu.make_async_copy(src, dst, sems.at[k]) for k, (src, dst) in enumerate(pairs)]
    for copy in copies:
        copy.start()
    return copies


def bin_edges(ref, b, bins, repeats):
    return jnp.concatenate(
        [ref[:, (g * bins + b) * TILE : (g * bins + b + 1) * TILE] for g in range(repeats)], axis=1
    )


def bin_indicators(src_ref, slot_ref, b, bins, repeats, slots):
    src = bin_edges(src_ref, b, bins, repeats) & (TILE - 1)
    slot = bin_edges(slot_ref, b, bins, repeats)
    row = lax.broadcasted_iota(jnp.int32, (TILE, src.shape[1]), 0)
    source = mask(row == src).astype(F8)
    low = mask(row == (slot & (TILE - 1)))
    high = slot >> 7
    return source, [(low * mask(high == h)).astype(F8) for h in range(slots // TILE)]


def scatter_kernel(
    counts_hbm, rows_hbm, src_hbm, slot_hbm, feats_hbm, out_hbm, out_ref, adj_ref, counts_ref, rows_ref, src_ref, slot_ref, feats_ref, sems, out_sems
):
    copies = start_all(
        [
            (src_hbm, src_ref),
            (slot_hbm, slot_ref),
            (feats_hbm, feats_ref),
            (rows_hbm, rows_ref),
            (counts_hbm, counts_ref),
        ],
        sems,
    )
    slots, verts = adj_ref.shape
    peers, cap = rows_ref.shape[1:]
    bins = verts // TILE
    repeats = src_ref.shape[1] // verts
    copies[0].wait()
    copies[1].wait()
    for b in range(bins):
        source, blocks = bin_indicators(src_ref, slot_ref, b, bins, repeats, slots)
        for h, block in enumerate(blocks):
            adj_ref[h * TILE : (h + 1) * TILE, b * TILE : (b + 1) * TILE] = dot(block, source, NT).astype(BF)
    for copy in copies[2:]:
        copy.wait()
    sub = lax.broadcasted_iota(jnp.int32, (INDEX_ROWS, cap), 0)
    slot_in_peer = lax.broadcasted_iota(jnp.int32, (cap, 2 * TILE), 0)
    outs = []
    step = peers // GATHER_STEPS
    for first in range(0, peers, step):
        rows = dot(adj_ref[first * cap : (first + step) * cap, :], feats_ref[...], NN)
        for q in range(first, first + step):
            part = rows[(q - first) * cap : (q - first + 1) * cap, :]
            part = jnp.where(slot_in_peer < counts_ref[0, q], part, 0.0).astype(BF)
            out_ref[q, 0:cap, :] = part[:, :TILE]
            out_ref[q, cap : 2 * cap, :] = part[:, TILE:]
            out_ref[q, 2 * cap :, :] = jnp.zeros((INDEX_ROWS, TILE), BF)
            index = rows_ref[0, q : q + 1, :]
            value = jnp.where(sub == 0, index >> 7, jnp.where(sub == 1, index & (TILE - 1), 0))
            out_ref[q, 2 * cap :, 0:cap] = value.astype(F32).astype(BF)
        those = pl.ds(first, step)
        copy = pltpu.make_async_copy(out_ref.at[those], out_hbm.at[those], out_sems.at[first // step])
        copy.start()
        outs.append(copy)
    for copy in outs:
        copy.wait()


def adjacency_kernel(src_hbm, slot_hbm, out_hbm, src_ref, slot_ref, adj_ref, sems, out_sems):
    copies = start_all([(src_hbm, src_ref), (slot_hbm, slot_ref)], sems)
    verts, slots = adj_ref.shape
    bins = verts // TILE
    repeats = src_ref.shape[1] // verts
    for copy in copies:
        copy.wait()
    outs = []
    per = ROWS // TILE
    for b in range(bins):
        source, blocks = bin_indicators(src_ref, slot_ref, b, bins, repeats, slots)
        for h, block in enumerate(blocks):
            adj_ref[b * TILE : (b + 1) * TILE, h * TILE : (h + 1) * TILE] = dot(source, block, NT).astype(BF)
        if b % per == per - 1:
            rows = pl.ds((b // per) * ROWS, ROWS)
            copy = pltpu.make_async_copy(adj_ref.at[rows], out_hbm.at[rows], out_sems.at[b // per])
            copy.start()
            outs.append(copy)
    for copy in outs:
        copy.wait()


def index_digits(cap, got_ref):
    peers = got_ref.shape[0]
    coded = got_ref[:, 2 * cap :, :].astype(F32).reshape(peers * INDEX_ROWS, TILE).astype(BF)
    pick_row = lax.broadcasted_iota(jnp.int32, (peers, peers * INDEX_ROWS), 1)
    pick_peer = lax.broadcasted_iota(jnp.int32, (peers, peers * INDEX_ROWS), 0) * INDEX_ROWS
    high = dot(mask(pick_row == pick_peer), coded, NN).astype(BF)
    low = dot(mask(pick_row == pick_peer + 1), coded, NN).astype(BF)
    return high, low


def master_kernel(
    cap,
    got_ref,
    ws_ref,
    wn_ref,
    adj_hbm,
    ages_hbm,
    feats_hbm,
    stale_hbm,
    cot_hbm,
    hidden_hbm,
    gp_hbm,
    agg_hbm,
    share_ref,
    arr_ref,
    ages_ref,
    feats_ref,
    stale_ref,
    cot_ref,
    hidden_ref,
    gp_ref,
    agg_ref,
    sems,
    out_sems,
):
    peers = got_ref.shape[0]
    verts, width = feats_ref.shape
    slots = peers * cap
    blocks = verts // ROWS
    copies = start_all(
        [(ages_hbm, ages_ref), (stale_hbm, stale_ref), (feats_hbm, feats_ref), (cot_hbm, cot_ref)], sems
    )
    high, low = index_digits(cap, got_ref)
    place = lax.broadcasted_iota(jnp.int32, (peers, cap, TILE), 1).reshape(slots, TILE)
    spread = mask(place == lax.broadcasted_iota(jnp.int32, (slots, TILE), 1))
    value = dot(high, spread, NT) * float(TILE) + dot(low, spread, NT)
    slot = lax.broadcasted_iota(jnp.int32, (peers, slots), 1)
    least = lax.broadcasted_iota(jnp.int32, (peers, slots), 0) * cap
    own = (slot >= least) & (slot < least + cap)
    row_index = jnp.sum(jnp.where(own, value, 0.0), axis=0, keepdims=True).astype(jnp.int32)
    sub = lax.broadcasted_iota(jnp.int32, (TILE, slots), 0)
    low_hot = mask(sub == (row_index & (TILE - 1)))
    row_high = row_index >> 7
    arr_ref[:, :TILE] = got_ref[:, 0:cap, :].reshape(slots, TILE)
    arr_ref[:, TILE:] = got_ref[:, cap : 2 * cap, :].reshape(slots, TILE)
    per = ROWS // TILE
    for block in range(blocks):
        hot = jnp.concatenate([low_hot * mask(row_high == block * per + k) for k in range(per)], axis=0)
        agg_ref[block * ROWS : (block + 1) * ROWS, :] = dot(hot, arr_ref[...], NN)
    for copy in copies:
        copy.wait()
    total = None
    outs = []
    fine = FINE // TILE
    for block in range(verts // FINE):
        rows = slice(block * FINE, (block + 1) * FINE)
        aged = []
        for k in range(block * fine, (block + 1) * fine):
            age = jnp.full((1, width), ages_ref[k], jnp.int32).astype(F32)
            aged.append(stale_ref[k * TILE : (k + 1) * TILE, :].astype(F32) * (1.0 / (1.0 + age)))
        agg = agg_ref[rows, :] + jnp.concatenate(aged, axis=0)
        agg_ref[rows, :] = agg
        inverse = lax.rsqrt(jnp.mean(agg * agg, axis=1, keepdims=True) + 1e-05)
        normed = (agg * inverse).astype(BF)
        feats = feats_ref[rows, :]
        pre = dot(feats, ws_ref[...], NN) + dot(normed, wn_ref[...], NN)
        sig = jax.nn.sigmoid(pre)
        hidden_ref[rows, :] = (pre * sig).astype(BF)
        gp = (cot_ref[rows, :].astype(F32) * sig * (1.0 + pre * (1.0 - sig))).astype(BF)
        gp_ref[rows, :] = gp
        part = pl.ds(block * FINE, FINE)
        for near, far in ((agg_ref, agg_hbm), (gp_ref, gp_hbm), (hidden_ref, hidden_hbm)):
            copy = pltpu.make_async_copy(near.at[part], far.at[part], out_sems.at[len(outs)])
            copy.start()
            outs.append(copy)
        grads = jnp.concatenate([dot(feats, gp, TN), dot(normed, gp, TN)], axis=0)
        total = grads if total is None else total + grads
    total = total.astype(BF)
    share = 2 * width // peers
    share_ref[:, :share, :] = total[:, :TILE].reshape(peers, share, TILE)
    share_ref[:, share:, :] = total[:, TILE:].reshape(peers, share, TILE)
    for copy in outs:
        copy.wait()


def outgoing_kernel(cap, got_ref, wn_ref, gp_hbm, agg_hbm, out_ref, gp_ref, agg_ref, ga_ref, sems):
    peers = got_ref.shape[0]
    verts = gp_ref.shape[0]
    slots = peers * cap
    parts = [pl.ds(block * ROWS, ROWS) for block in range(verts // ROWS)]
    copies = start_all(
        [(far.at[part], near.at[part]) for part in parts for far, near in ((gp_hbm, gp_ref), (agg_hbm, agg_ref))],
        sems,
    )
    for block in range(verts // ROWS):
        rows = slice(block * ROWS, (block + 1) * ROWS)
        copies[2 * block].wait()
        copies[2 * block + 1].wait()
        agg = agg_ref[rows, :]
        inverse = lax.rsqrt(jnp.mean(agg * agg, axis=1, keepdims=True) + 1e-05)
        gn = dot(gp_ref[rows, :], wn_ref[...], NT)
        inner = jnp.mean(gn * agg, axis=1, keepdims=True)
        ga_ref[rows, :] = (inverse * (gn - agg * (inverse * inverse * inner))).astype(BF)
    high, low = index_digits(cap, got_ref)
    place = lax.broadcasted_iota(jnp.int32, (peers, cap, TILE), 1).reshape(slots, TILE)
    peer = lax.broadcasted_iota(jnp.int32, (peers, cap, TILE), 0).reshape(slots, TILE)
    lane = lax.broadcasted_iota(jnp.int32, (slots, TILE), 1)
    at_peer = mask(peer == lane)[:, :peers]
    value = dot(at_peer, high, NN) * float(TILE) + dot(at_peer, low, NN)
    index = jnp.sum(jnp.where(place == lane, value, 0.0), axis=1, keepdims=True).astype(jnp.int32)
    step = peers // GATHER_STEPS
    for first in range(0, peers, step):
        part = slice(first * cap, (first + step) * cap)
        lanes = lax.broadcasted_iota(jnp.int32, (step * cap, verts), 1)
        rows = dot(mask(lanes == index[part, :]), ga_ref[...], NN).astype(BF)
        out_ref[first : first + step, 0:cap, :] = rows[:, :TILE].reshape(step, cap, TILE)
        out_ref[first : first + step, cap:, :] = rows[:, TILE:].reshape(step, cap, TILE)


def sum_kernel(parts_ref, after_hbm, out_ref):
    out_ref[...] = jnp.sum(parts_ref[...].astype(F32), axis=0)


def share_kernel(own_ref, near_ref, far_ref, across_ref, after_hbm, out_ref):
    total = (own_ref[...] + near_ref[...]) + (far_ref[...] + across_ref[...])
    out_ref[...] = jnp.broadcast_to(total.astype(BF)[None], out_ref.shape)


def back_kernel(
    cap, got_ref, gp_ref, ws_ref, counts_hbm, adj_hbm, out_hbm, counts_ref, adj_ref, grad_ref, out_ref, sems, out_sems
):
    parts = [pl.ds(block * ROWS, ROWS) for block in range(out_ref.shape[0] // ROWS)]
    copies = start_all(
        [(counts_hbm, counts_ref)] + [(adj_hbm.at[part], adj_ref.at[part]) for part in parts], sems
    )
    copies[0].wait()
    slot_in_peer = lax.broadcasted_iota(jnp.int32, (cap, TILE), 0)
    for q in range(got_ref.shape[0]):
        live = slot_in_peer < counts_ref[0, q]
        for half in range(2):
            rows = got_ref[q, half * cap : (half + 1) * cap, :]
            grad_ref[q * cap : (q + 1) * cap, half * TILE : (half + 1) * TILE] = jnp.where(
                live, rows.astype(F32), 0.0
            ).astype(BF)
    outs = []
    for block, part in enumerate(parts):
        rows = slice(block * ROWS, (block + 1) * ROWS)
        own = dot(gp_ref[rows, :], ws_ref[...], NT)
        copies[1 + block].wait()
        out_ref[rows, :] = (dot(adj_ref[rows, :], grad_ref[...], NN) + own).astype(BF)
        copy = pltpu.make_async_copy(out_ref.at[part], out_hbm.at[part], out_sems.at[block])
        copy.start()
        outs.append(copy)
    for copy in outs:
        copy.wait()


def update_kernel(sum_ref, ws_ref, wn_ref, new_s_ref, new_n_ref):
    peers, share = sum_ref.shape[0], sum_ref.shape[1] // 2
    left = sum_ref[:, :share, :].astype(F32).reshape(peers * share, TILE)
    right = sum_ref[:, share:, :].astype(F32).reshape(peers * share, TILE)
    total = jnp.concatenate([left, right], axis=1)
    norm = jnp.sqrt(jnp.sum(total * total, keepdims=True))
    scale = 8.0 * jnp.minimum(1.0, 1.0 / norm)
    half = new_s_ref.shape[0]
    new_s_ref[...] = ws_ref[...].astype(F32) - scale * total[:half]
    new_n_ref[...] = wn_ref[...].astype(F32) - scale * total[half:]


HBM = pl.BlockSpec(memory_space=pltpu.HBM)
VMEM = pl.BlockSpec(memory_space=pltpu.VMEM)


def call(kernel, name, args, near, outs, out_near, scratch=(), flops=10**9, limit=56):
    size = sum(a.size * a.dtype.itemsize for a in args)
    return pl.pallas_call(
        kernel,
        name=name,
        in_specs=[VMEM if k < near else HBM for k in range(len(args))],
        out_specs=[VMEM if k in out_near else HBM for k in range(len(outs))],
        out_shape=outs,
        scratch_shapes=list(scratch),
        compiler_params=pltpu.CompilerParams(vmem_limit_bytes=limit * MIB),
        cost_estimate=pl.CostEstimate(flops=flops, bytes_accessed=size, transcendentals=0),
    )(*args)


def shape(dims, dtype=BF):
    return jax.ShapeDtypeStruct(dims, dtype)


def like(x):
    return pltpu.VMEM(x.shape, x.dtype)


def scatter(slot_counts, replica_row, edge_src, edge_slot, feats):
    peers, cap = replica_row.shape[1:]
    return call(
        scatter_kernel,
        "scatter",
        (slot_counts, replica_row, edge_src, edge_slot, feats),
        0,
        [shape((peers, 2 * cap + INDEX_ROWS, TILE))],
        (),
        [
            pltpu.VMEM((peers, 2 * cap + INDEX_ROWS, TILE), BF),
            pltpu.VMEM((peers * cap, feats.shape[0]), BF),
            pltpu.SMEM(slot_counts.shape, jnp.int32),
            like(replica_row),
            like(edge_src),
            like(edge_slot),
            like(feats),
            pltpu.SemaphoreType.DMA((5,)),
            pltpu.SemaphoreType.DMA((GATHER_STEPS,)),
        ],
    )[0]


def adjacency(edge_src, edge_slot, verts, slots):
    return call(
        adjacency_kernel,
        "adjacency",
        (edge_src, edge_slot),
        0,
        [shape((verts, slots))],
        (),
        [
            like(edge_src),
            like(edge_slot),
            pltpu.VMEM((verts, slots), BF),
            pltpu.SemaphoreType.DMA((2,)),
            pltpu.SemaphoreType.DMA((verts // ROWS,)),
        ],
        flops=6 * 10**9,
    )[0]


def masters(cap, got, adj, ages, feats, stale, cot, ws, wn):
    verts, width = feats.shape
    peers = got.shape[0]
    share = 2 * width // peers
    return call(
        functools.partial(master_kernel, cap),
        "masters",
        (got, ws, wn, adj, ages, feats, stale, cot),
        3,
        [
            shape((verts, width)),
            shape((verts, width)),
            shape((verts, width), F32),
            shape((peers, 2 * share, TILE)),
        ],
        (3,),
        [
            pltpu.VMEM((peers * cap, width), BF),
            pltpu.SMEM(ages.shape, jnp.int32),
            like(feats),
            like(stale),
            like(cot),
            like(feats),
            like(feats),
            pltpu.VMEM((verts, width), F32),
            pltpu.SemaphoreType.DMA((4,)),
            pltpu.SemaphoreType.DMA((3 * (verts // FINE),)),
        ],
        limit=52,
    )


def outgoing(cap, got, gp, agg, wn):
    return call(
        functools.partial(outgoing_kernel, cap),
        "outgoing",
        (got, wn, gp, agg),
        2,
        [shape((got.shape[0], 2 * cap, TILE))],
        (0,),
        [like(gp), like(agg), like(gp), pltpu.SemaphoreType.DMA((2 * (gp.shape[0] // ROWS),))],
        limit=52,
    )[0]


def summed(parts, after):
    return call(sum_kernel, "summed", (parts, after), 1, [shape(parts.shape[1:], F32)], (0,), flops=10**6, limit=16)[0]


def shares(parts, after):
    peers = after.shape[0]
    return call(
        share_kernel, "shares", (*parts, after), 4, [shape((peers,) + parts[0].shape)], (0,), flops=10**6, limit=16
    )[0]


def back(cap, got, gp, slot_counts, adj, ws):
    blocks = gp.shape[0] // ROWS
    return call(
        functools.partial(back_kernel, cap),
        "back",
        (got, gp, ws, slot_counts, adj),
        3,
        [shape(gp.shape)],
        (),
        [
            pltpu.SMEM(slot_counts.shape, jnp.int32),
            like(adj),
            pltpu.VMEM((got.shape[0] * cap, gp.shape[1]), BF),
            like(gp),
            pltpu.SemaphoreType.DMA((1 + blocks,)),
            pltpu.SemaphoreType.DMA((blocks,)),
        ],
        limit=50,
    )[0]


def update(sums, ws, wn):
    return call(update_kernel, "update", (sums, ws, wn), 3, [shape(ws.shape, F32)] * 2, (0, 1), limit=16)


def exchange(x):
    return lax.all_to_all(x, "dom", split_axis=0, concat_axis=0, tiled=True)


def body(
    feats, edge_src, edge_slot, slot_counts, replica_row, stale_agg, bin_ages, cotangent, w_self, w_neigh
):
    verts, width = feats.shape
    peers, cap = replica_row.shape[1:]
    arrived = exchange(scatter(slot_counts, replica_row, edge_src, edge_slot, feats))
    adj = adjacency(edge_src, edge_slot, verts, peers * cap)
    hidden, grad_pre, aggregate, parts = masters(
        cap, arrived, adj, bin_ages, feats, stale_agg, cotangent, w_self, w_neigh
    )
    parts = exchange(parts)
    sent = outgoing(cap, arrived, grad_pre, aggregate, w_neigh)
    own = summed(parts, sent)
    groups = range(lax.axis_size("group"))
    others = [lax.ppermute(own, "group", [(k, k ^ other) for k in groups]) for other in (1, 2, 3)]
    returned = exchange(sent)
    sums = exchange(shares((own, *others), returned))
    feat_grad = back(cap, returned, grad_pre, slot_counts, adj, w_self)
    new_self, new_neigh = update(sums, w_self, w_neigh)
    return (hidden, feat_grad, new_self, new_neigh)


def solution(mesh):
    both = ("group", "dom")
    wide = P(both, None)
    placed = (wide, wide, wide, wide, P(both, None, None), wide, P(both), wide, P(), P())
    return jax.shard_map(
        body,
        mesh=mesh,
        in_specs=placed,
        out_specs=(wide, wide, P(), P()),
        check_vma=False,
    )
```

```python
import functools

import jax
import jax.numpy as jnp
from jax import lax
from jax.experimental import pallas as pl
from jax.experimental.pallas import tpu as pltpu
from jax.sharding import PartitionSpec as P

BF = jnp.bfloat16
F8 = jnp.float8_e4m3fn
F32 = jnp.float32
TILE = 128
ROWS = 512
FINE = 256
INDEX_ROWS = 8
GATHER_STEPS = 4
NN = (((1,), (0,)), ((), ()))
NT = (((1,), (1,)), ((), ()))
TN = (((0,), (0,)), ((), ()))
MIB = 1024 * 1024


def dot(a, b, dims):
    return lax.dot_general(a, b, dims, preferred_element_type=F32)


def mask(cond):
    return jnp.where(cond, 1.0, 0.0).astype(BF)


def mask16(cond):
    return jnp.where(cond, jnp.ones((), BF), jnp.zeros((), BF))


def start_all(pairs, sems):
    copies = [pltpu.make_async_copy(src, dst, sems.at[k]) for k, (src, dst) in enumerate(pairs)]
    for copy in copies:
        copy.start()
    return copies


def bin_edges(ref, b, bins, repeats):
    return jnp.concatenate(
        [ref[:, (g * bins + b) * TILE : (g * bins + b + 1) * TILE] for g in range(repeats)], axis=1
    )


def bin_indicators(src_ref, slot_ref, b, bins, repeats, slots):
    src = bin_edges(src_ref, b, bins, repeats) & (TILE - 1)
    slot = bin_edges(slot_ref, b, bins, repeats)
    row = lax.broadcasted_iota(jnp.int16, (TILE, src.shape[1]), 0)
    source = mask16(row == src.astype(jnp.int16)).astype(F8)
    low = mask16(row == (slot & (TILE - 1)).astype(jnp.int16))
    high = slot >> 7
    return source, [(low * mask(high == h)).astype(F8) for h in range(slots // TILE)]


def scatter_kernel(
    counts_hbm, rows_hbm, src_hbm, slot_hbm, feats_hbm, out_hbm, out_ref, adj_ref, counts_ref, rows_ref, src_ref, slot_ref, feats_ref, sems, out_sems
):
    copies = start_all(
        [
            (src_hbm, src_ref),
            (slot_hbm, slot_ref),
            (feats_hbm, feats_ref),
            (rows_hbm, rows_ref),
            (counts_hbm, counts_ref),
        ],
        sems,
    )
    slots, verts = adj_ref.shape
    peers, cap = rows_ref.shape[1:]
    bins = verts // TILE
    repeats = src_ref.shape[1] // verts
    copies[0].wait()
    copies[1].wait()
    for b in range(bins):
        source, blocks = bin_indicators(src_ref, slot_ref, b, bins, repeats, slots)
        for h, block in enumerate(blocks):
            adj_ref[h * TILE : (h + 1) * TILE, b * TILE : (b + 1) * TILE] = dot(block, source, NT).astype(BF)
    for copy in copies[2:]:
        copy.wait()
    sub = lax.broadcasted_iota(jnp.int32, (INDEX_ROWS, cap), 0)
    slot_in_peer = lax.broadcasted_iota(jnp.int32, (cap, 2 * TILE), 0)
    outs = []
    step = peers // GATHER_STEPS
    for first in range(0, peers, step):
        rows = dot(adj_ref[first * cap : (first + step) * cap, :], feats_ref[...], NN)
        for q in range(first, first + step):
            part = rows[(q - first) * cap : (q - first + 1) * cap, :]
            part = jnp.where(slot_in_peer < counts_ref[0, q], part, 0.0).astype(BF)
            out_ref[q, 0:cap, :] = part[:, :TILE]
            out_ref[q, cap : 2 * cap, :] = part[:, TILE:]
            out_ref[q, 2 * cap :, :] = jnp.zeros((INDEX_ROWS, TILE), BF)
            index = rows_ref[0, q : q + 1, :]
            value = jnp.where(sub == 0, index >> 7, jnp.where(sub == 1, index & (TILE - 1), 0))
            out_ref[q, 2 * cap :, 0:cap] = value.astype(F32).astype(BF)
        those = pl.ds(first, step)
        copy = pltpu.make_async_copy(out_ref.at[those], out_hbm.at[those], out_sems.at[first // step])
        copy.start()
        outs.append(copy)
    for copy in outs:
        copy.wait()


def adjacency_kernel(src_hbm, slot_hbm, out_hbm, src_ref, slot_ref, adj_ref, sems, out_sems):
    copies = start_all([(src_hbm, src_ref), (slot_hbm, slot_ref)], sems)
    verts, slots = adj_ref.shape
    bins = verts // TILE
    repeats = src_ref.shape[1] // verts
    for copy in copies:
        copy.wait()
    outs = []
    per = ROWS // TILE
    for b in range(bins):
        source, blocks = bin_indicators(src_ref, slot_ref, b, bins, repeats, slots)
        for h, block in enumerate(blocks):
            adj_ref[b * TILE : (b + 1) * TILE, h * TILE : (h + 1) * TILE] = dot(source, block, NT).astype(BF)
        if b % per == per - 1:
            rows = pl.ds((b // per) * ROWS, ROWS)
            copy = pltpu.make_async_copy(adj_ref.at[rows], out_hbm.at[rows], out_sems.at[b // per])
            copy.start()
            outs.append(copy)
    for copy in outs:
        copy.wait()


def index_digits(cap, got_ref):
    peers = got_ref.shape[0]
    coded = got_ref[:, 2 * cap :, :].astype(F32).reshape(peers * INDEX_ROWS, TILE).astype(BF)
    pick_row = lax.broadcasted_iota(jnp.int32, (peers, peers * INDEX_ROWS), 1)
    pick_peer = lax.broadcasted_iota(jnp.int32, (peers, peers * INDEX_ROWS), 0) * INDEX_ROWS
    high = dot(mask(pick_row == pick_peer), coded, NN).astype(BF)
    low = dot(mask(pick_row == pick_peer + 1), coded, NN).astype(BF)
    return high, low


def master_kernel(
    cap,
    got_ref,
    ws_ref,
    wn_ref,
    adj_hbm,
    ages_hbm,
    feats_hbm,
    stale_hbm,
    cot_hbm,
    hidden_hbm,
    gp_hbm,
    agg_hbm,
    share_ref,
    arr_ref,
    ages_ref,
    feats_ref,
    stale_ref,
    cot_ref,
    hidden_ref,
    gp_ref,
    agg_ref,
    sems,
    out_sems,
):
    peers = got_ref.shape[0]
    verts, width = feats_ref.shape
    slots = peers * cap
    blocks = verts // ROWS
    copies = start_all(
        [(ages_hbm, ages_ref), (stale_hbm, stale_ref), (feats_hbm, feats_ref), (cot_hbm, cot_ref)], sems
    )
    high, low = index_digits(cap, got_ref)
    place = lax.broadcasted_iota(jnp.int32, (peers, cap, TILE), 1).reshape(slots, TILE)
    spread = mask(place == lax.broadcasted_iota(jnp.int32, (slots, TILE), 1))
    value = dot(high, spread, NT) * float(TILE) + dot(low, spread, NT)
    slot = lax.broadcasted_iota(jnp.int32, (peers, slots), 1)
    least = lax.broadcasted_iota(jnp.int32, (peers, slots), 0) * cap
    own = (slot >= least) & (slot < least + cap)
    row_index = jnp.sum(jnp.where(own, value, 0.0), axis=0, keepdims=True).astype(jnp.int32)
    sub = lax.broadcasted_iota(jnp.int16, (TILE, slots), 0)
    low_hot = mask16(sub == (row_index & (TILE - 1)).astype(jnp.int16))
    row_high = row_index >> 7
    arr_ref[:, :TILE] = got_ref[:, 0:cap, :].reshape(slots, TILE)
    arr_ref[:, TILE:] = got_ref[:, cap : 2 * cap, :].reshape(slots, TILE)
    per = ROWS // TILE
    for block in range(blocks):
        hot = jnp.concatenate([low_hot * mask(row_high == block * per + k) for k in range(per)], axis=0)
        agg_ref[block * ROWS : (block + 1) * ROWS, :] = dot(hot, arr_ref[...], NN)
    for copy in copies:
        copy.wait()
    total = None
    outs = []
    fine = FINE // TILE
    for block in range(verts // FINE):
        rows = slice(block * FINE, (block + 1) * FINE)
        aged = []
        for k in range(block * fine, (block + 1) * fine):
            age = jnp.full((1, width), ages_ref[k], jnp.int32).astype(F32)
            aged.append(stale_ref[k * TILE : (k + 1) * TILE, :].astype(F32) * (1.0 / (1.0 + age)))
        agg = agg_ref[rows, :] + jnp.concatenate(aged, axis=0)
        agg_ref[rows, :] = agg
        inverse = lax.rsqrt(jnp.mean(agg * agg, axis=1, keepdims=True) + 1e-05)
        normed = (agg * inverse).astype(BF)
        feats = feats_ref[rows, :]
        pre = dot(feats, ws_ref[...], NN) + dot(normed, wn_ref[...], NN)
        sig = jax.nn.sigmoid(pre)
        hidden_ref[rows, :] = (pre * sig).astype(BF)
        gp = (cot_ref[rows, :].astype(F32) * sig * (1.0 + pre * (1.0 - sig))).astype(BF)
        gp_ref[rows, :] = gp
        part = pl.ds(block * FINE, FINE)
        for near, far in ((agg_ref, agg_hbm), (gp_ref, gp_hbm), (hidden_ref, hidden_hbm)):
            copy = pltpu.make_async_copy(near.at[part], far.at[part], out_sems.at[len(outs)])
            copy.start()
            outs.append(copy)
        grads = jnp.concatenate([dot(feats, gp, TN), dot(normed, gp, TN)], axis=0)
        total = grads if total is None else total + grads
    total = total.astype(BF)
    share = 2 * width // peers
    share_ref[:, :share, :] = total[:, :TILE].reshape(peers, share, TILE)
    share_ref[:, share:, :] = total[:, TILE:].reshape(peers, share, TILE)
    for copy in outs:
        copy.wait()


def outgoing_kernel(cap, got_ref, wn_ref, gp_hbm, agg_hbm, out_ref, gp_ref, agg_ref, ga_ref, sems):
    peers = got_ref.shape[0]
    verts = gp_ref.shape[0]
    slots = peers * cap
    parts = [pl.ds(block * ROWS, ROWS) for block in range(verts // ROWS)]
    copies = start_all(
        [(far.at[part], near.at[part]) for part in parts for far, near in ((gp_hbm, gp_ref), (agg_hbm, agg_ref))],
        sems,
    )
    for block in range(verts // ROWS):
        rows = slice(block * ROWS, (block + 1) * ROWS)
        copies[2 * block].wait()
        copies[2 * block + 1].wait()
        agg = agg_ref[rows, :]
        inverse = lax.rsqrt(jnp.mean(agg * agg, axis=1, keepdims=True) + 1e-05)
        gn = dot(gp_ref[rows, :], wn_ref[...], NT)
        inner = jnp.mean(gn * agg, axis=1, keepdims=True)
        ga_ref[rows, :] = (inverse * (gn - agg * (inverse * inverse * inner))).astype(BF)
    high, low = index_digits(cap, got_ref)
    place = lax.broadcasted_iota(jnp.int32, (peers, cap, TILE), 1).reshape(slots, TILE)
    peer = lax.broadcasted_iota(jnp.int32, (peers, cap, TILE), 0).reshape(slots, TILE)
    lane = lax.broadcasted_iota(jnp.int32, (slots, TILE), 1)
    at_peer = mask(peer == lane)[:, :peers]
    value = dot(at_peer, high, NN) * float(TILE) + dot(at_peer, low, NN)
    index = jnp.sum(jnp.where(place == lane, value, 0.0), axis=1, keepdims=True).astype(jnp.int32)
    step = peers // GATHER_STEPS
    for first in range(0, peers, step):
        part = slice(first * cap, (first + step) * cap)
        lanes = lax.broadcasted_iota(jnp.int16, (step * cap, verts), 1)
        rows = dot(mask16(lanes == index[part, :].astype(jnp.int16)), ga_ref[...], NN).astype(BF)
        out_ref[first : first + step, 0:cap, :] = rows[:, :TILE].reshape(step, cap, TILE)
        out_ref[first : first + step, cap:, :] = rows[:, TILE:].reshape(step, cap, TILE)


def sum_kernel(parts_ref, after_hbm, out_ref):
    out_ref[...] = jnp.sum(parts_ref[...].astype(F32), axis=0)


def tie_kernel(values_hbm, after_hbm, out_hbm):
    pass


def share_kernel(own_ref, near_ref, far_ref, across_ref, out_ref):
    total = (own_ref[...] + near_ref[...]) + (far_ref[...] + across_ref[...])
    out_ref[...] = jnp.broadcast_to(total.astype(BF)[None], out_ref.shape)


def back_kernel(
    cap, got_ref, gp_ref, ws_ref, counts_hbm, adj_hbm, out_hbm, counts_ref, adj_ref, grad_ref, out_ref, sems, out_sems
):
    parts = [pl.ds(block * ROWS, ROWS) for block in range(out_ref.shape[0] // ROWS)]
    copies = start_all(
        [(counts_hbm, counts_ref)] + [(adj_hbm.at[part], adj_ref.at[part]) for part in parts], sems
    )
    copies[0].wait()
    slot_in_peer = lax.broadcasted_iota(jnp.int32, (cap, TILE), 0)
    for q in range(got_ref.shape[0]):
        live = slot_in_peer < counts_ref[0, q]
        for half in range(2):
            rows = got_ref[q, half * cap : (half + 1) * cap, :]
            grad_ref[q * cap : (q + 1) * cap, half * TILE : (half + 1) * TILE] = jnp.where(
                live, rows.astype(F32), 0.0
            ).astype(BF)
    outs = []
    for block, part in enumerate(parts):
        rows = slice(block * ROWS, (block + 1) * ROWS)
        own = dot(gp_ref[rows, :], ws_ref[...], NT)
        copies[1 + block].wait()
        out_ref[rows, :] = (dot(adj_ref[rows, :], grad_ref[...], NN) + own).astype(BF)
        copy = pltpu.make_async_copy(out_ref.at[part], out_hbm.at[part], out_sems.at[block])
        copy.start()
        outs.append(copy)
    for copy in outs:
        copy.wait()


def update_kernel(sum_ref, ws_ref, wn_ref, new_s_ref, new_n_ref):
    peers, share = sum_ref.shape[0], sum_ref.shape[1] // 2
    left = sum_ref[:, :share, :].astype(F32).reshape(peers * share, TILE)
    right = sum_ref[:, share:, :].astype(F32).reshape(peers * share, TILE)
    total = jnp.concatenate([left, right], axis=1)
    norm = jnp.sqrt(jnp.sum(total * total, keepdims=True))
    scale = 8.0 * jnp.minimum(1.0, 1.0 / norm)
    half = new_s_ref.shape[0]
    new_s_ref[...] = ws_ref[...].astype(F32) - scale * total[:half]
    new_n_ref[...] = wn_ref[...].astype(F32) - scale * total[half:]


HBM = pl.BlockSpec(memory_space=pltpu.HBM)
VMEM = pl.BlockSpec(memory_space=pltpu.VMEM)


def call(kernel, name, args, near, outs, out_near, scratch=(), flops=10**9, limit=56):
    size = sum(a.size * a.dtype.itemsize for a in args)
    return pl.pallas_call(
        kernel,
        name=name,
        in_specs=[VMEM if k < near else HBM for k in range(len(args))],
        out_specs=[VMEM if k in out_near else HBM for k in range(len(outs))],
        out_shape=outs,
        scratch_shapes=list(scratch),
        compiler_params=pltpu.CompilerParams(vmem_limit_bytes=limit * MIB),
        cost_estimate=pl.CostEstimate(flops=flops, bytes_accessed=size, transcendentals=0),
    )(*args)


def shape(dims, dtype=BF):
    return jax.ShapeDtypeStruct(dims, dtype)


def like(x):
    return pltpu.VMEM(x.shape, x.dtype)


def scatter(slot_counts, replica_row, edge_src, edge_slot, feats):
    peers, cap = replica_row.shape[1:]
    return call(
        scatter_kernel,
        "scatter",
        (slot_counts, replica_row, edge_src, edge_slot, feats),
        0,
        [shape((peers, 2 * cap + INDEX_ROWS, TILE))],
        (),
        [
            pltpu.VMEM((peers, 2 * cap + INDEX_ROWS, TILE), BF),
            pltpu.VMEM((peers * cap, feats.shape[0]), BF),
            pltpu.SMEM(slot_counts.shape, jnp.int32),
            like(replica_row),
            like(edge_src),
            like(edge_slot),
            like(feats),
            pltpu.SemaphoreType.DMA((5,)),
            pltpu.SemaphoreType.DMA((GATHER_STEPS,)),
        ],
    )[0]


def adjacency(edge_src, edge_slot, verts, slots):
    return call(
        adjacency_kernel,
        "adjacency",
        (edge_src, edge_slot),
        0,
        [shape((verts, slots))],
        (),
        [
            like(edge_src),
            like(edge_slot),
            pltpu.VMEM((verts, slots), BF),
            pltpu.SemaphoreType.DMA((2,)),
            pltpu.SemaphoreType.DMA((verts // ROWS,)),
        ],
        flops=6 * 10**9,
    )[0]


def masters(cap, got, adj, ages, feats, stale, cot, ws, wn):
    verts, width = feats.shape
    peers = got.shape[0]
    share = 2 * width // peers
    return call(
        functools.partial(master_kernel, cap),
        "masters",
        (got, ws, wn, adj, ages, feats, stale, cot),
        3,
        [
            shape((verts, width)),
            shape((verts, width)),
            shape((verts, width), F32),
            shape((peers, 2 * share, TILE)),
        ],
        (3,),
        [
            pltpu.VMEM((peers * cap, width), BF),
            pltpu.SMEM(ages.shape, jnp.int32),
            like(feats),
            like(stale),
            like(cot),
            like(feats),
            like(feats),
            pltpu.VMEM((verts, width), F32),
            pltpu.SemaphoreType.DMA((4,)),
            pltpu.SemaphoreType.DMA((3 * (verts // FINE),)),
        ],
        limit=52,
    )


def outgoing(cap, got, gp, agg, wn):
    return call(
        functools.partial(outgoing_kernel, cap),
        "outgoing",
        (got, wn, gp, agg),
        2,
        [shape((got.shape[0], 2 * cap, TILE))],
        (0,),
        [like(gp), like(agg), like(gp), pltpu.SemaphoreType.DMA((2 * (gp.shape[0] // ROWS),))],
        limit=52,
    )[0]


def summed(parts, after):
    return call(sum_kernel, "summed", (parts, after), 1, [shape(parts.shape[1:], F32)], (0,), flops=10**6, limit=16)[0]


def shares(parts, peers):
    return call(share_kernel, "shares", parts, 4, [shape((peers,) + parts[0].shape)], (0,), flops=10**6, limit=16)[0]


def tied(values, after):
    return pl.pallas_call(
        tie_kernel,
        name="tied",
        in_specs=[HBM, HBM],
        out_specs=HBM,
        out_shape=shape(values.shape),
        input_output_aliases={0: 0},
        compiler_params=pltpu.CompilerParams(vmem_limit_bytes=16 * MIB),
        cost_estimate=pl.CostEstimate(flops=0, bytes_accessed=0, transcendentals=0),
    )(values, after)


def back(cap, got, gp, slot_counts, adj, ws):
    blocks = gp.shape[0] // ROWS
    return call(
        functools.partial(back_kernel, cap),
        "back",
        (got, gp, ws, slot_counts, adj),
        3,
        [shape(gp.shape)],
        (),
        [
            pltpu.SMEM(slot_counts.shape, jnp.int32),
            like(adj),
            pltpu.VMEM((got.shape[0] * cap, gp.shape[1]), BF),
            like(gp),
            pltpu.SemaphoreType.DMA((1 + blocks,)),
            pltpu.SemaphoreType.DMA((blocks,)),
        ],
        limit=50,
    )[0]


def update(sums, ws, wn):
    return call(update_kernel, "update", (sums, ws, wn), 3, [shape(ws.shape, F32)] * 2, (0, 1), limit=16)


def exchange(x):
    return lax.all_to_all(x, "dom", split_axis=0, concat_axis=0, tiled=True)


def body(
    feats, edge_src, edge_slot, slot_counts, replica_row, stale_agg, bin_ages, cotangent, w_self, w_neigh
):
    verts, width = feats.shape
    peers, cap = replica_row.shape[1:]
    arrived = exchange(scatter(slot_counts, replica_row, edge_src, edge_slot, feats))
    adj = adjacency(edge_src, edge_slot, verts, peers * cap)
    hidden, grad_pre, aggregate, parts = masters(
        cap, arrived, adj, bin_ages, feats, stale_agg, cotangent, w_self, w_neigh
    )
    parts = exchange(parts)
    sent = outgoing(cap, arrived, grad_pre, aggregate, w_neigh)
    own = summed(parts, sent)
    groups = range(lax.axis_size("group"))
    others = [lax.ppermute(own, "group", [(k, k ^ other) for k in groups]) for other in (1, 2, 3)]
    returned = exchange(sent)
    sums = exchange(tied(shares((own, *others), peers), returned))
    feat_grad = back(cap, returned, grad_pre, slot_counts, adj, w_self)
    new_self, new_neigh = update(sums, w_self, w_neigh)
    return (hidden, feat_grad, new_self, new_neigh)


def solution(mesh):
    both = ("group", "dom")
    wide = P(both, None)
    placed = (wide, wide, wide, wide, P(both, None, None), wide, P(both), wide, P(), P())
    return jax.shard_map(
        body,
        mesh=mesh,
        in_specs=placed,
        out_specs=(wide, wide, P(), P()),
        check_vma=False,
    )
```

```python
import functools

import jax
import jax.numpy as jnp
from jax import lax
from jax.experimental import pallas as pl
from jax.experimental.pallas import tpu as pltpu
from jax.sharding import PartitionSpec as P

BF = jnp.bfloat16
F8 = jnp.float8_e4m3fn
F32 = jnp.float32
TILE = 128
ROWS = 512
FINE = 256
INDEX_ROWS = 16
GATHER_STEPS = 4
NN = (((1,), (0,)), ((), ()))
NT = (((1,), (1,)), ((), ()))
TN = (((0,), (0,)), ((), ()))
MIB = 1024 * 1024


def dot(a, b, dims):
    return lax.dot_general(a, b, dims, preferred_element_type=F32)


def mask(cond):
    return jnp.where(cond, 1.0, 0.0).astype(BF)


def mask16(cond):
    return jnp.where(cond, jnp.ones((), BF), jnp.zeros((), BF))


def start_all(pairs, sems):
    copies = [pltpu.make_async_copy(src, dst, sems.at[k]) for k, (src, dst) in enumerate(pairs)]
    for copy in copies:
        copy.start()
    return copies


def bin_edges(ref, b, bins, repeats):
    return jnp.concatenate(
        [ref[:, (g * bins + b) * TILE : (g * bins + b + 1) * TILE] for g in range(repeats)], axis=1
    )


def bin_indicators(src_ref, slot_ref, b, bins, repeats, slots):
    src = bin_edges(src_ref, b, bins, repeats) & (TILE - 1)
    slot = bin_edges(slot_ref, b, bins, repeats)
    row = lax.broadcasted_iota(jnp.int16, (TILE, src.shape[1]), 0)
    source = mask16(row == src.astype(jnp.int16)).astype(F8)
    low = mask16(row == (slot & (TILE - 1)).astype(jnp.int16))
    high = slot >> 7
    return source, [(low * mask(high == h)).astype(F8) for h in range(slots // TILE)]


def scatter_kernel(
    counts_hbm, rows_hbm, src_hbm, slot_hbm, feats_hbm, out_hbm, out_ref, adj_ref, counts_ref, rows_ref, src_ref, slot_ref, feats_ref, sems, out_sems
):
    copies = start_all(
        [
            (src_hbm, src_ref),
            (slot_hbm, slot_ref),
            (feats_hbm, feats_ref),
            (rows_hbm, rows_ref),
            (counts_hbm, counts_ref),
        ],
        sems,
    )
    slots, verts = adj_ref.shape
    peers, cap = rows_ref.shape[1:]
    bins = verts // TILE
    repeats = src_ref.shape[1] // verts
    copies[0].wait()
    copies[1].wait()
    for b in range(bins):
        source, blocks = bin_indicators(src_ref, slot_ref, b, bins, repeats, slots)
        for h, block in enumerate(blocks):
            adj_ref[h * TILE : (h + 1) * TILE, b * TILE : (b + 1) * TILE] = dot(block, source, NT).astype(BF)
    for copy in copies[2:]:
        copy.wait()
    sub = lax.broadcasted_iota(jnp.int32, (INDEX_ROWS, cap), 0)
    slot_in_peer = lax.broadcasted_iota(jnp.int32, (cap, 2 * TILE), 0)
    outs = []
    step = peers // GATHER_STEPS
    for first in range(0, peers, step):
        rows = dot(adj_ref[first * cap : (first + step) * cap, :], feats_ref[...], NN)
        for q in range(first, first + step):
            part = rows[(q - first) * cap : (q - first + 1) * cap, :]
            part = jnp.where(slot_in_peer < counts_ref[0, q], part, 0.0).astype(BF)
            out_ref[q, 0:cap, :] = part[:, :TILE]
            out_ref[q, cap : 2 * cap, :] = part[:, TILE:]
            out_ref[q, 2 * cap :, :] = jnp.zeros((INDEX_ROWS, TILE), BF)
            index = rows_ref[0, q : q + 1, :]
            value = jnp.where(sub == 0, index >> 7, jnp.where(sub == 1, index & (TILE - 1), 0))
            out_ref[q, 2 * cap :, 0:cap] = value.astype(F32).astype(BF)
        those = pl.ds(first, step)
        copy = pltpu.make_async_copy(out_ref.at[those], out_hbm.at[those], out_sems.at[first // step])
        copy.start()
        outs.append(copy)
    for copy in outs:
        copy.wait()


def adjacency_kernel(src_hbm, slot_hbm, out_hbm, src_ref, slot_ref, adj_ref, sems, out_sems):
    copies = start_all([(src_hbm, src_ref), (slot_hbm, slot_ref)], sems)
    verts, slots = adj_ref.shape
    bins = verts // TILE
    repeats = src_ref.shape[1] // verts
    for copy in copies:
        copy.wait()
    outs = []
    per = ROWS // TILE
    for b in range(bins):
        source, blocks = bin_indicators(src_ref, slot_ref, b, bins, repeats, slots)
        for h, block in enumerate(blocks):
            adj_ref[b * TILE : (b + 1) * TILE, h * TILE : (h + 1) * TILE] = dot(source, block, NT).astype(BF)
        if b % per == per - 1:
            rows = pl.ds((b // per) * ROWS, ROWS)
            copy = pltpu.make_async_copy(adj_ref.at[rows], out_hbm.at[rows], out_sems.at[b // per])
            copy.start()
            outs.append(copy)
    for copy in outs:
        copy.wait()


def index_digits(cap, got_ref):
    peers = got_ref.shape[0]
    coded = got_ref[:, 2 * cap :, :].reshape(peers * INDEX_ROWS, TILE)
    pick_row = lax.broadcasted_iota(jnp.int32, (peers, peers * INDEX_ROWS), 1)
    pick_peer = lax.broadcasted_iota(jnp.int32, (peers, peers * INDEX_ROWS), 0) * INDEX_ROWS
    high = dot(mask(pick_row == pick_peer), coded, NN).astype(BF)
    low = dot(mask(pick_row == pick_peer + 1), coded, NN).astype(BF)
    return high, low


def master_kernel(
    cap,
    got_ref,
    ws_ref,
    wn_ref,
    adj_hbm,
    ages_hbm,
    feats_hbm,
    stale_hbm,
    cot_hbm,
    hidden_hbm,
    gp_hbm,
    agg_hbm,
    share_ref,
    arr_ref,
    ages_ref,
    feats_ref,
    stale_ref,
    cot_ref,
    hidden_ref,
    gp_ref,
    agg_ref,
    sems,
    out_sems,
):
    peers = got_ref.shape[0]
    verts, width = feats_ref.shape
    slots = peers * cap
    blocks = verts // ROWS
    copies = start_all(
        [(ages_hbm, ages_ref), (stale_hbm, stale_ref), (feats_hbm, feats_ref), (cot_hbm, cot_ref)], sems
    )
    high, low = index_digits(cap, got_ref)
    place = lax.broadcasted_iota(jnp.int32, (peers, cap, TILE), 1).reshape(slots, TILE)
    spread = mask(place == lax.broadcasted_iota(jnp.int32, (slots, TILE), 1))
    value = dot(high, spread, NT) * float(TILE) + dot(low, spread, NT)
    slot = lax.broadcasted_iota(jnp.int32, (peers, slots), 1)
    least = lax.broadcasted_iota(jnp.int32, (peers, slots), 0) * cap
    own = (slot >= least) & (slot < least + cap)
    row_index = jnp.sum(jnp.where(own, value, 0.0), axis=0, keepdims=True).astype(jnp.int32)
    sub = lax.broadcasted_iota(jnp.int16, (TILE, slots), 0)
    low_hot = mask16(sub == (row_index & (TILE - 1)).astype(jnp.int16))
    row_high = row_index >> 7
    arr_ref[:, :TILE] = got_ref[:, 0:cap, :].reshape(slots, TILE)
    arr_ref[:, TILE:] = got_ref[:, cap : 2 * cap, :].reshape(slots, TILE)
    per = ROWS // TILE
    for block in range(blocks):
        hot = jnp.concatenate([low_hot * mask(row_high == block * per + k) for k in range(per)], axis=0)
        agg_ref[block * ROWS : (block + 1) * ROWS, :] = dot(hot, arr_ref[...], NN)
    for copy in copies:
        copy.wait()
    total = None
    outs = []
    fine = FINE // TILE
    for block in range(verts // FINE):
        rows = slice(block * FINE, (block + 1) * FINE)
        aged = []
        for k in range(block * fine, (block + 1) * fine):
            age = jnp.full((1, width), ages_ref[k], jnp.int32).astype(F32)
            aged.append(stale_ref[k * TILE : (k + 1) * TILE, :].astype(F32) * (1.0 / (1.0 + age)))
        agg = agg_ref[rows, :] + jnp.concatenate(aged, axis=0)
        agg_ref[rows, :] = agg
        inverse = lax.rsqrt(jnp.mean(agg * agg, axis=1, keepdims=True) + 1e-05)
        normed = (agg * inverse).astype(BF)
        feats = feats_ref[rows, :]
        pre = dot(feats, ws_ref[...], NN) + dot(normed, wn_ref[...], NN)
        sig = jax.nn.sigmoid(pre)
        hidden_ref[rows, :] = (pre * sig).astype(BF)
        gp = (cot_ref[rows, :].astype(F32) * sig * (1.0 + pre * (1.0 - sig))).astype(BF)
        gp_ref[rows, :] = gp
        part = pl.ds(block * FINE, FINE)
        for near, far in ((agg_ref, agg_hbm), (gp_ref, gp_hbm), (hidden_ref, hidden_hbm)):
            copy = pltpu.make_async_copy(near.at[part], far.at[part], out_sems.at[len(outs)])
            copy.start()
            outs.append(copy)
        grads = jnp.concatenate([dot(feats, gp, TN), dot(normed, gp, TN)], axis=0)
        total = grads if total is None else total + grads
    total = total.astype(BF)
    share = 2 * width // peers
    share_ref[:, :share, :] = total[:, :TILE].reshape(peers, share, TILE)
    share_ref[:, share:, :] = total[:, TILE:].reshape(peers, share, TILE)
    for copy in outs:
        copy.wait()


def outgoing_kernel(cap, got_ref, wn_ref, gp_hbm, agg_hbm, out_ref, gp_ref, agg_ref, ga_ref, sems):
    peers = got_ref.shape[0]
    verts = gp_ref.shape[0]
    slots = peers * cap
    parts = [pl.ds(block * ROWS, ROWS) for block in range(verts // ROWS)]
    copies = start_all(
        [(far.at[part], near.at[part]) for part in parts for far, near in ((gp_hbm, gp_ref), (agg_hbm, agg_ref))],
        sems,
    )
    for block in range(verts // ROWS):
        rows = slice(block * ROWS, (block + 1) * ROWS)
        copies[2 * block].wait()
        copies[2 * block + 1].wait()
        agg = agg_ref[rows, :]
        inverse = lax.rsqrt(jnp.mean(agg * agg, axis=1, keepdims=True) + 1e-05)
        gn = dot(gp_ref[rows, :], wn_ref[...], NT)
        inner = jnp.mean(gn * agg, axis=1, keepdims=True)
        ga_ref[rows, :] = (inverse * (gn - agg * (inverse * inverse * inner))).astype(BF)
    high, low = index_digits(cap, got_ref)
    place = lax.broadcasted_iota(jnp.int32, (peers, cap, TILE), 1).reshape(slots, TILE)
    peer = lax.broadcasted_iota(jnp.int32, (peers, cap, TILE), 0).reshape(slots, TILE)
    lane = lax.broadcasted_iota(jnp.int32, (slots, TILE), 1)
    at_peer = mask(peer == lane)[:, :peers]
    value = dot(at_peer, high, NN) * float(TILE) + dot(at_peer, low, NN)
    index = jnp.sum(jnp.where(place == lane, value, 0.0), axis=1, keepdims=True).astype(jnp.int32)
    step = peers // GATHER_STEPS
    for first in range(0, peers, step):
        part = slice(first * cap, (first + step) * cap)
        lanes = lax.broadcasted_iota(jnp.int16, (step * cap, verts), 1)
        rows = dot(mask16(lanes == index[part, :].astype(jnp.int16)), ga_ref[...], NN).astype(BF)
        out_ref[first : first + step, 0:cap, :] = rows[:, :TILE].reshape(step, cap, TILE)
        out_ref[first : first + step, cap:, :] = rows[:, TILE:].reshape(step, cap, TILE)


def sum_kernel(parts_ref, after_hbm, out_ref):
    out_ref[...] = jnp.sum(parts_ref[...].astype(F32), axis=0)


def tie_kernel(values_hbm, after_hbm, out_hbm):
    pass


def share_kernel(own_ref, near_ref, far_ref, across_ref, out_ref):
    total = (own_ref[...] + near_ref[...]) + (far_ref[...] + across_ref[...])
    out_ref[...] = jnp.broadcast_to(total.astype(BF)[None], out_ref.shape)


def back_kernel(
    cap, got_ref, gp_ref, ws_ref, counts_hbm, adj_hbm, out_hbm, counts_ref, adj_ref, grad_ref, out_ref, sems, out_sems
):
    parts = [pl.ds(block * ROWS, ROWS) for block in range(out_ref.shape[0] // ROWS)]
    copies = start_all(
        [(counts_hbm, counts_ref)] + [(adj_hbm.at[part], adj_ref.at[part]) for part in parts], sems
    )
    copies[0].wait()
    slot_in_peer = lax.broadcasted_iota(jnp.int32, (cap, TILE), 0)
    for q in range(got_ref.shape[0]):
        live = slot_in_peer < counts_ref[0, q]
        for half in range(2):
            rows = got_ref[q, half * cap : (half + 1) * cap, :]
            grad_ref[q * cap : (q + 1) * cap, half * TILE : (half + 1) * TILE] = jnp.where(
                live, rows.astype(F32), 0.0
            ).astype(BF)
    outs = []
    for block, part in enumerate(parts):
        rows = slice(block * ROWS, (block + 1) * ROWS)
        own = dot(gp_ref[rows, :], ws_ref[...], NT)
        copies[1 + block].wait()
        out_ref[rows, :] = (dot(adj_ref[rows, :], grad_ref[...], NN) + own).astype(BF)
        copy = pltpu.make_async_copy(out_ref.at[part], out_hbm.at[part], out_sems.at[block])
        copy.start()
        outs.append(copy)
    for copy in outs:
        copy.wait()


def update_kernel(sum_ref, ws_ref, wn_ref, new_s_ref, new_n_ref):
    peers, share = sum_ref.shape[0], sum_ref.shape[1] // 2
    left = sum_ref[:, :share, :].astype(F32).reshape(peers * share, TILE)
    right = sum_ref[:, share:, :].astype(F32).reshape(peers * share, TILE)
    total = jnp.concatenate([left, right], axis=1)
    norm = jnp.sqrt(jnp.sum(total * total, keepdims=True))
    scale = 8.0 * jnp.minimum(1.0, 1.0 / norm)
    half = new_s_ref.shape[0]
    new_s_ref[...] = ws_ref[...].astype(F32) - scale * total[:half]
    new_n_ref[...] = wn_ref[...].astype(F32) - scale * total[half:]


HBM = pl.BlockSpec(memory_space=pltpu.HBM)
VMEM = pl.BlockSpec(memory_space=pltpu.VMEM)


def call(kernel, name, args, near, outs, out_near, scratch=(), flops=10**9, limit=56):
    size = sum(a.size * a.dtype.itemsize for a in args)
    return pl.pallas_call(
        kernel,
        name=name,
        in_specs=[VMEM if k < near else HBM for k in range(len(args))],
        out_specs=[VMEM if k in out_near else HBM for k in range(len(outs))],
        out_shape=outs,
        scratch_shapes=list(scratch),
        compiler_params=pltpu.CompilerParams(vmem_limit_bytes=limit * MIB),
        cost_estimate=pl.CostEstimate(flops=flops, bytes_accessed=size, transcendentals=0),
    )(*args)


def shape(dims, dtype=BF):
    return jax.ShapeDtypeStruct(dims, dtype)


def like(x):
    return pltpu.VMEM(x.shape, x.dtype)


def scatter(slot_counts, replica_row, edge_src, edge_slot, feats):
    peers, cap = replica_row.shape[1:]
    return call(
        scatter_kernel,
        "scatter",
        (slot_counts, replica_row, edge_src, edge_slot, feats),
        0,
        [shape((peers, 2 * cap + INDEX_ROWS, TILE))],
        (),
        [
            pltpu.VMEM((peers, 2 * cap + INDEX_ROWS, TILE), BF),
            pltpu.VMEM((peers * cap, feats.shape[0]), BF),
            pltpu.SMEM(slot_counts.shape, jnp.int32),
            like(replica_row),
            like(edge_src),
            like(edge_slot),
            like(feats),
            pltpu.SemaphoreType.DMA((5,)),
            pltpu.SemaphoreType.DMA((GATHER_STEPS,)),
        ],
    )[0]


def adjacency(edge_src, edge_slot, verts, slots):
    return call(
        adjacency_kernel,
        "adjacency",
        (edge_src, edge_slot),
        0,
        [shape((verts, slots))],
        (),
        [
            like(edge_src),
            like(edge_slot),
            pltpu.VMEM((verts, slots), BF),
            pltpu.SemaphoreType.DMA((2,)),
            pltpu.SemaphoreType.DMA((verts // ROWS,)),
        ],
        flops=6 * 10**9,
    )[0]


def masters(cap, got, adj, ages, feats, stale, cot, ws, wn):
    verts, width = feats.shape
    peers = got.shape[0]
    share = 2 * width // peers
    return call(
        functools.partial(master_kernel, cap),
        "masters",
        (got, ws, wn, adj, ages, feats, stale, cot),
        3,
        [
            shape((verts, width)),
            shape((verts, width)),
            shape((verts, width), F32),
            shape((peers, 2 * share, TILE)),
        ],
        (3,),
        [
            pltpu.VMEM((peers * cap, width), BF),
            pltpu.SMEM(ages.shape, jnp.int32),
            like(feats),
            like(stale),
            like(cot),
            like(feats),
            like(feats),
            pltpu.VMEM((verts, width), F32),
            pltpu.SemaphoreType.DMA((4,)),
            pltpu.SemaphoreType.DMA((3 * (verts // FINE),)),
        ],
        limit=52,
    )


def outgoing(cap, got, gp, agg, wn):
    return call(
        functools.partial(outgoing_kernel, cap),
        "outgoing",
        (got, wn, gp, agg),
        2,
        [shape((got.shape[0], 2 * cap, TILE))],
        (0,),
        [like(gp), like(agg), like(gp), pltpu.SemaphoreType.DMA((2 * (gp.shape[0] // ROWS),))],
        limit=52,
    )[0]


def summed(parts, after):
    return call(sum_kernel, "summed", (parts, after), 1, [shape(parts.shape[1:], F32)], (0,), flops=10**6, limit=16)[0]


def shares(parts, peers):
    return call(share_kernel, "shares", parts, 4, [shape((peers,) + parts[0].shape)], (0,), flops=10**6, limit=16)[0]


def tied(values, after):
    return pl.pallas_call(
        tie_kernel,
        name="tied",
        in_specs=[HBM, HBM],
        out_specs=HBM,
        out_shape=shape(values.shape),
        input_output_aliases={0: 0},
        compiler_params=pltpu.CompilerParams(vmem_limit_bytes=16 * MIB),
        cost_estimate=pl.CostEstimate(flops=0, bytes_accessed=0, transcendentals=0),
    )(values, after)


def back(cap, got, gp, slot_counts, adj, ws):
    blocks = gp.shape[0] // ROWS
    return call(
        functools.partial(back_kernel, cap),
        "back",
        (got, gp, ws, slot_counts, adj),
        3,
        [shape(gp.shape)],
        (),
        [
            pltpu.SMEM(slot_counts.shape, jnp.int32),
            like(adj),
            pltpu.VMEM((got.shape[0] * cap, gp.shape[1]), BF),
            like(gp),
            pltpu.SemaphoreType.DMA((1 + blocks,)),
            pltpu.SemaphoreType.DMA((blocks,)),
        ],
        limit=50,
    )[0]


def update(sums, ws, wn):
    return call(update_kernel, "update", (sums, ws, wn), 3, [shape(ws.shape, F32)] * 2, (0, 1), limit=16)


def exchange(x):
    return lax.all_to_all(x, "dom", split_axis=0, concat_axis=0, tiled=True)


def body(
    feats, edge_src, edge_slot, slot_counts, replica_row, stale_agg, bin_ages, cotangent, w_self, w_neigh
):
    verts, width = feats.shape
    peers, cap = replica_row.shape[1:]
    arrived = exchange(scatter(slot_counts, replica_row, edge_src, edge_slot, feats))
    adj = adjacency(edge_src, edge_slot, verts, peers * cap)
    hidden, grad_pre, aggregate, parts = masters(
        cap, arrived, adj, bin_ages, feats, stale_agg, cotangent, w_self, w_neigh
    )
    parts = exchange(parts)
    sent = outgoing(cap, arrived, grad_pre, aggregate, w_neigh)
    own = summed(parts, sent)
    groups = range(lax.axis_size("group"))
    others = [lax.ppermute(own, "group", [(k, k ^ other) for k in groups]) for other in (1, 2, 3)]
    returned = exchange(sent)
    sums = exchange(tied(shares((own, *others), peers), returned))
    feat_grad = back(cap, returned, grad_pre, slot_counts, adj, w_self)
    new_self, new_neigh = update(sums, w_self, w_neigh)
    return (hidden, feat_grad, new_self, new_neigh)


def solution(mesh):
    both = ("group", "dom")
    wide = P(both, None)
    placed = (wide, wide, wide, wide, P(both, None, None), wide, P(both), wide, P(), P())
    return jax.shard_map(
        body,
        mesh=mesh,
        in_specs=placed,
        out_specs=(wide, wide, P(), P()),
        check_vma=False,
    )
```

```python
import functools

import jax
import jax.numpy as jnp
from jax import lax
from jax.experimental import pallas as pl
from jax.experimental.pallas import tpu as pltpu
from jax.sharding import PartitionSpec as P

BF = jnp.bfloat16
F8 = jnp.float8_e4m3fn
F32 = jnp.float32
TILE = 128
ROWS = 512
FINE = 256
INDEX_ROWS = 16
GATHER_STEPS = 4
NN = (((1,), (0,)), ((), ()))
NT = (((1,), (1,)), ((), ()))
TN = (((0,), (0,)), ((), ()))
MIB = 1024 * 1024


def dot(a, b, dims):
    return lax.dot_general(a, b, dims, preferred_element_type=F32)


def mask(cond):
    return jnp.where(cond, 1.0, 0.0).astype(BF)


def mask16(cond):
    return jnp.where(cond, jnp.ones((), BF), jnp.zeros((), BF))


def start_all(pairs, sems):
    copies = [pltpu.make_async_copy(src, dst, sems.at[k]) for k, (src, dst) in enumerate(pairs)]
    for copy in copies:
        copy.start()
    return copies


def bin_edges(ref, b, bins, repeats):
    return jnp.concatenate(
        [ref[:, (g * bins + b) * TILE : (g * bins + b + 1) * TILE] for g in range(repeats)], axis=1
    )


def bin_indicators(src_ref, slot_ref, b, bins, repeats, slots):
    src = bin_edges(src_ref, b, bins, repeats) & (TILE - 1)
    slot = bin_edges(slot_ref, b, bins, repeats)
    row = lax.broadcasted_iota(jnp.int16, (TILE, src.shape[1]), 0)
    source = mask16(row == src.astype(jnp.int16)).astype(F8)
    low = mask16(row == (slot & (TILE - 1)).astype(jnp.int16))
    high = slot >> 7
    return source, [(low * mask(high == h)).astype(F8) for h in range(slots // TILE)]


def scatter_kernel(
    counts_hbm, rows_hbm, src_hbm, slot_hbm, feats_hbm, out_hbm, out_ref, adj_ref, counts_ref, rows_ref, src_ref, slot_ref, feats_ref, sems, out_sems
):
    copies = start_all(
        [
            (src_hbm, src_ref),
            (slot_hbm, slot_ref),
            (feats_hbm, feats_ref),
            (rows_hbm, rows_ref),
            (counts_hbm, counts_ref),
        ],
        sems,
    )
    slots, verts = adj_ref.shape
    peers, cap = rows_ref.shape[1:]
    bins = verts // TILE
    repeats = src_ref.shape[1] // verts
    copies[0].wait()
    copies[1].wait()
    for b in range(bins):
        source, blocks = bin_indicators(src_ref, slot_ref, b, bins, repeats, slots)
        for h, block in enumerate(blocks):
            adj_ref[h * TILE : (h + 1) * TILE, b * TILE : (b + 1) * TILE] = dot(block, source, NT).astype(BF)
    for copy in copies[2:]:
        copy.wait()
    sub = lax.broadcasted_iota(jnp.int32, (INDEX_ROWS, cap), 0)
    slot_in_peer = lax.broadcasted_iota(jnp.int32, (cap, 2 * TILE), 0)
    outs = []
    step = peers // GATHER_STEPS
    for first in range(0, peers, step):
        rows = dot(adj_ref[first * cap : (first + step) * cap, :], feats_ref[...], NN)
        for q in range(first, first + step):
            part = rows[(q - first) * cap : (q - first + 1) * cap, :]
            part = jnp.where(slot_in_peer < counts_ref[0, q], part, 0.0).astype(BF)
            out_ref[q, 0:cap, :] = part[:, :TILE]
            out_ref[q, cap : 2 * cap, :] = part[:, TILE:]
            out_ref[q, 2 * cap :, :] = jnp.zeros((INDEX_ROWS, TILE), BF)
            index = rows_ref[0, q : q + 1, :]
            value = jnp.where(sub == 0, index >> 7, jnp.where(sub == 1, index & (TILE - 1), 0))
            out_ref[q, 2 * cap :, 0:cap] = value.astype(F32).astype(BF)
        those = pl.ds(first, step)
        copy = pltpu.make_async_copy(out_ref.at[those], out_hbm.at[those], out_sems.at[first // step])
        copy.start()
        outs.append(copy)
    for copy in outs:
        copy.wait()


def adjacency_kernel(src_hbm, slot_hbm, out_hbm, src_ref, slot_ref, adj_ref, sems, out_sems):
    copies = start_all([(src_hbm, src_ref), (slot_hbm, slot_ref)], sems)
    verts, slots = adj_ref.shape
    bins = verts // TILE
    repeats = src_ref.shape[1] // verts
    for copy in copies:
        copy.wait()
    outs = []
    per = ROWS // TILE
    for b in range(bins):
        source, blocks = bin_indicators(src_ref, slot_ref, b, bins, repeats, slots)
        for h, block in enumerate(blocks):
            adj_ref[b * TILE : (b + 1) * TILE, h * TILE : (h + 1) * TILE] = dot(source, block, NT).astype(BF)
        if b % per == per - 1:
            rows = pl.ds((b // per) * ROWS, ROWS)
            copy = pltpu.make_async_copy(adj_ref.at[rows], out_hbm.at[rows], out_sems.at[b // per])
            copy.start()
            outs.append(copy)
    for copy in outs:
        copy.wait()


def index_digits(cap, got_ref):
    peers = got_ref.shape[0]
    coded = got_ref[:, 2 * cap :, :].reshape(peers * INDEX_ROWS, TILE)
    pick_row = lax.broadcasted_iota(jnp.int32, (peers, peers * INDEX_ROWS), 1)
    pick_peer = lax.broadcasted_iota(jnp.int32, (peers, peers * INDEX_ROWS), 0) * INDEX_ROWS
    high = dot(mask(pick_row == pick_peer), coded, NN).astype(BF)
    low = dot(mask(pick_row == pick_peer + 1), coded, NN).astype(BF)
    return high, low


def master_kernel(
    cap,
    got_ref,
    ws_ref,
    wn_ref,
    adj_hbm,
    ages_hbm,
    feats_hbm,
    stale_hbm,
    cot_hbm,
    hidden_hbm,
    gp_hbm,
    agg_hbm,
    share_hbm,
    arr_ref,
    ages_ref,
    feats_ref,
    stale_ref,
    cot_ref,
    hidden_ref,
    gp_ref,
    agg_ref,
    share_ref,
    sems,
    out_sems,
):
    peers = got_ref.shape[0]
    verts, width = feats_ref.shape
    slots = peers * cap
    blocks = verts // ROWS
    copies = start_all(
        [(ages_hbm, ages_ref), (stale_hbm, stale_ref), (feats_hbm, feats_ref), (cot_hbm, cot_ref)], sems
    )
    high, low = index_digits(cap, got_ref)
    place = lax.broadcasted_iota(jnp.int32, (peers, cap, TILE), 1).reshape(slots, TILE)
    spread = mask(place == lax.broadcasted_iota(jnp.int32, (slots, TILE), 1))
    value = dot(high, spread, NT) * float(TILE) + dot(low, spread, NT)
    slot = lax.broadcasted_iota(jnp.int32, (peers, slots), 1)
    least = lax.broadcasted_iota(jnp.int32, (peers, slots), 0) * cap
    own = (slot >= least) & (slot < least + cap)
    row_index = jnp.sum(jnp.where(own, value, 0.0), axis=0, keepdims=True).astype(jnp.int32)
    sub = lax.broadcasted_iota(jnp.int16, (TILE, slots), 0)
    low_hot = mask16(sub == (row_index & (TILE - 1)).astype(jnp.int16))
    row_high = row_index >> 7
    arr_ref[:, :TILE] = got_ref[:, 0:cap, :].reshape(slots, TILE)
    arr_ref[:, TILE:] = got_ref[:, cap : 2 * cap, :].reshape(slots, TILE)
    per = ROWS // TILE
    for block in range(blocks):
        hot = jnp.concatenate([low_hot * mask(row_high == block * per + k) for k in range(per)], axis=0)
        agg_ref[block * ROWS : (block + 1) * ROWS, :] = dot(hot, arr_ref[...], NN)
    for copy in copies:
        copy.wait()
    total = None
    outs = []
    fine = FINE // TILE
    for block in range(verts // FINE):
        rows = slice(block * FINE, (block + 1) * FINE)
        aged = []
        for k in range(block * fine, (block + 1) * fine):
            age = jnp.full((1, width), ages_ref[k], jnp.int32).astype(F32)
            aged.append(stale_ref[k * TILE : (k + 1) * TILE, :].astype(F32) * (1.0 / (1.0 + age)))
        agg = agg_ref[rows, :] + jnp.concatenate(aged, axis=0)
        agg_ref[rows, :] = agg
        inverse = lax.rsqrt(jnp.mean(agg * agg, axis=1, keepdims=True) + 1e-05)
        normed = (agg * inverse).astype(BF)
        feats = feats_ref[rows, :]
        pre = dot(feats, ws_ref[...], NN) + dot(normed, wn_ref[...], NN)
        sig = jax.nn.sigmoid(pre)
        hidden_ref[rows, :] = (pre * sig).astype(BF)
        gp = (cot_ref[rows, :].astype(F32) * sig * (1.0 + pre * (1.0 - sig))).astype(BF)
        gp_ref[rows, :] = gp
        part = pl.ds(block * FINE, FINE)
        for near, far in ((agg_ref, agg_hbm), (gp_ref, gp_hbm), (hidden_ref, hidden_hbm)):
            copy = pltpu.make_async_copy(near.at[part], far.at[part], out_sems.at[len(outs)])
            copy.start()
            outs.append(copy)
        grads = jnp.concatenate([dot(feats, gp, TN), dot(normed, gp, TN)], axis=0)
        total = grads if total is None else total + grads
    total = total.astype(BF)
    share = 2 * width // peers
    share_ref[:, :share, :] = total[:, :TILE].reshape(peers, share, TILE)
    share_ref[:, share:, :] = total[:, TILE:].reshape(peers, share, TILE)
    copy = pltpu.make_async_copy(share_ref, share_hbm, out_sems.at[len(outs)])
    copy.start()
    outs.append(copy)
    for copy in outs:
        copy.wait()


def outgoing_kernel(cap, got_ref, wn_ref, gp_hbm, agg_hbm, out_ref, gp_ref, agg_ref, ga_ref, sems):
    peers = got_ref.shape[0]
    verts = gp_ref.shape[0]
    slots = peers * cap
    parts = [pl.ds(block * ROWS, ROWS) for block in range(verts // ROWS)]
    copies = start_all(
        [(far.at[part], near.at[part]) for part in parts for far, near in ((gp_hbm, gp_ref), (agg_hbm, agg_ref))],
        sems,
    )
    for block in range(verts // ROWS):
        rows = slice(block * ROWS, (block + 1) * ROWS)
        copies[2 * block].wait()
        copies[2 * block + 1].wait()
        agg = agg_ref[rows, :]
        inverse = lax.rsqrt(jnp.mean(agg * agg, axis=1, keepdims=True) + 1e-05)
        gn = dot(gp_ref[rows, :], wn_ref[...], NT)
        inner = jnp.mean(gn * agg, axis=1, keepdims=True)
        ga_ref[rows, :] = (inverse * (gn - agg * (inverse * inverse * inner))).astype(BF)
    high, low = index_digits(cap, got_ref)
    place = lax.broadcasted_iota(jnp.int32, (peers, cap, TILE), 1).reshape(slots, TILE)
    peer = lax.broadcasted_iota(jnp.int32, (peers, cap, TILE), 0).reshape(slots, TILE)
    lane = lax.broadcasted_iota(jnp.int32, (slots, TILE), 1)
    at_peer = mask(peer == lane)[:, :peers]
    value = dot(at_peer, high, NN) * float(TILE) + dot(at_peer, low, NN)
    index = jnp.sum(jnp.where(place == lane, value, 0.0), axis=1, keepdims=True).astype(jnp.int32)
    step = peers // GATHER_STEPS
    for first in range(0, peers, step):
        part = slice(first * cap, (first + step) * cap)
        lanes = lax.broadcasted_iota(jnp.int16, (step * cap, verts), 1)
        rows = dot(mask16(lanes == index[part, :].astype(jnp.int16)), ga_ref[...], NN).astype(BF)
        out_ref[first : first + step, 0:cap, :] = rows[:, :TILE].reshape(step, cap, TILE)
        out_ref[first : first + step, cap:, :] = rows[:, TILE:].reshape(step, cap, TILE)


def sum_kernel(parts_ref, after_hbm, out_ref):
    out_ref[...] = jnp.sum(parts_ref[...].astype(F32), axis=0)


def tie_kernel(values_hbm, after_hbm, out_hbm):
    pass


def share_kernel(own_ref, near_ref, far_ref, across_ref, out_ref):
    total = (own_ref[...] + near_ref[...]) + (far_ref[...] + across_ref[...])
    out_ref[...] = jnp.broadcast_to(total.astype(BF)[None], out_ref.shape)


def back_kernel(
    cap, got_ref, gp_ref, ws_ref, counts_hbm, adj_hbm, out_hbm, counts_ref, adj_ref, grad_ref, out_ref, sems, out_sems
):
    parts = [pl.ds(block * ROWS, ROWS) for block in range(out_ref.shape[0] // ROWS)]
    copies = start_all(
        [(counts_hbm, counts_ref)] + [(adj_hbm.at[part], adj_ref.at[part]) for part in parts], sems
    )
    copies[0].wait()
    slot_in_peer = lax.broadcasted_iota(jnp.int32, (cap, TILE), 0)
    for q in range(got_ref.shape[0]):
        live = slot_in_peer < counts_ref[0, q]
        for half in range(2):
            rows = got_ref[q, half * cap : (half + 1) * cap, :]
            grad_ref[q * cap : (q + 1) * cap, half * TILE : (half + 1) * TILE] = jnp.where(
                live, rows.astype(F32), 0.0
            ).astype(BF)
    outs = []
    for block, part in enumerate(parts):
        rows = slice(block * ROWS, (block + 1) * ROWS)
        own = dot(gp_ref[rows, :], ws_ref[...], NT)
        copies[1 + block].wait()
        out_ref[rows, :] = (dot(adj_ref[rows, :], grad_ref[...], NN) + own).astype(BF)
        copy = pltpu.make_async_copy(out_ref.at[part], out_hbm.at[part], out_sems.at[block])
        copy.start()
        outs.append(copy)
    for copy in outs:
        copy.wait()


def update_kernel(sum_ref, ws_ref, wn_ref, new_s_ref, new_n_ref):
    peers, share = sum_ref.shape[0], sum_ref.shape[1] // 2
    left = sum_ref[:, :share, :].astype(F32).reshape(peers * share, TILE)
    right = sum_ref[:, share:, :].astype(F32).reshape(peers * share, TILE)
    total = jnp.concatenate([left, right], axis=1)
    norm = jnp.sqrt(jnp.sum(total * total, keepdims=True))
    scale = 8.0 * jnp.minimum(1.0, 1.0 / norm)
    half = new_s_ref.shape[0]
    new_s_ref[...] = ws_ref[...].astype(F32) - scale * total[:half]
    new_n_ref[...] = wn_ref[...].astype(F32) - scale * total[half:]


HBM = pl.BlockSpec(memory_space=pltpu.HBM)
VMEM = pl.BlockSpec(memory_space=pltpu.VMEM)


def call(kernel, name, args, near, outs, out_near, scratch=(), flops=10**9, limit=56):
    size = sum(a.size * a.dtype.itemsize for a in args)
    return pl.pallas_call(
        kernel,
        name=name,
        in_specs=[VMEM if k < near else HBM for k in range(len(args))],
        out_specs=[VMEM if k in out_near else HBM for k in range(len(outs))],
        out_shape=outs,
        scratch_shapes=list(scratch),
        compiler_params=pltpu.CompilerParams(vmem_limit_bytes=limit * MIB),
        cost_estimate=pl.CostEstimate(flops=flops, bytes_accessed=size, transcendentals=0),
    )(*args)


def shape(dims, dtype=BF):
    return jax.ShapeDtypeStruct(dims, dtype)


def like(x):
    return pltpu.VMEM(x.shape, x.dtype)


def scatter(slot_counts, replica_row, edge_src, edge_slot, feats):
    peers, cap = replica_row.shape[1:]
    return call(
        scatter_kernel,
        "scatter",
        (slot_counts, replica_row, edge_src, edge_slot, feats),
        0,
        [shape((peers, 2 * cap + INDEX_ROWS, TILE))],
        (),
        [
            pltpu.VMEM((peers, 2 * cap + INDEX_ROWS, TILE), BF),
            pltpu.VMEM((peers * cap, feats.shape[0]), BF),
            pltpu.SMEM(slot_counts.shape, jnp.int32),
            like(replica_row),
            like(edge_src),
            like(edge_slot),
            like(feats),
            pltpu.SemaphoreType.DMA((5,)),
            pltpu.SemaphoreType.DMA((GATHER_STEPS,)),
        ],
    )[0]


def adjacency(edge_src, edge_slot, verts, slots):
    return call(
        adjacency_kernel,
        "adjacency",
        (edge_src, edge_slot),
        0,
        [shape((verts, slots))],
        (),
        [
            like(edge_src),
            like(edge_slot),
            pltpu.VMEM((verts, slots), BF),
            pltpu.SemaphoreType.DMA((2,)),
            pltpu.SemaphoreType.DMA((verts // ROWS,)),
        ],
        flops=6 * 10**9,
    )[0]


def masters(cap, got, adj, ages, feats, stale, cot, ws, wn):
    verts, width = feats.shape
    peers = got.shape[0]
    share = 2 * width // peers
    return call(
        functools.partial(master_kernel, cap),
        "masters",
        (got, ws, wn, adj, ages, feats, stale, cot),
        3,
        [
            shape((verts, width)),
            shape((verts, width)),
            shape((verts, width), F32),
            shape((peers, 2 * share, TILE)),
        ],
        (),
        [
            pltpu.VMEM((peers * cap, width), BF),
            pltpu.SMEM(ages.shape, jnp.int32),
            like(feats),
            like(stale),
            like(cot),
            like(feats),
            like(feats),
            pltpu.VMEM((verts, width), F32),
            pltpu.VMEM((peers, 2 * share, TILE), BF),
            pltpu.SemaphoreType.DMA((4,)),
            pltpu.SemaphoreType.DMA((3 * (verts // FINE) + 1,)),
        ],
        limit=52,
    )


def outgoing(cap, got, gp, agg, wn):
    return call(
        functools.partial(outgoing_kernel, cap),
        "outgoing",
        (got, wn, gp, agg),
        2,
        [shape((got.shape[0], 2 * cap, TILE))],
        (0,),
        [like(gp), like(agg), like(gp), pltpu.SemaphoreType.DMA((2 * (gp.shape[0] // ROWS),))],
        limit=52,
    )[0]


def summed(parts, after):
    return call(sum_kernel, "summed", (parts, after), 1, [shape(parts.shape[1:], F32)], (0,), flops=10**6, limit=16)[0]


def shares(parts, peers):
    return call(share_kernel, "shares", parts, 4, [shape((peers,) + parts[0].shape)], (0,), flops=10**6, limit=16)[0]


def tied(values, after):
    return pl.pallas_call(
        tie_kernel,
        name="tied",
        in_specs=[HBM, HBM],
        out_specs=HBM,
        out_shape=shape(values.shape),
        input_output_aliases={0: 0},
        compiler_params=pltpu.CompilerParams(vmem_limit_bytes=16 * MIB),
        cost_estimate=pl.CostEstimate(flops=0, bytes_accessed=0, transcendentals=0),
    )(values, after)


def back(cap, got, gp, slot_counts, adj, ws):
    blocks = gp.shape[0] // ROWS
    return call(
        functools.partial(back_kernel, cap),
        "back",
        (got, gp, ws, slot_counts, adj),
        3,
        [shape(gp.shape)],
        (),
        [
            pltpu.SMEM(slot_counts.shape, jnp.int32),
            like(adj),
            pltpu.VMEM((got.shape[0] * cap, gp.shape[1]), BF),
            like(gp),
            pltpu.SemaphoreType.DMA((1 + blocks,)),
            pltpu.SemaphoreType.DMA((blocks,)),
        ],
        limit=50,
    )[0]


def update(sums, ws, wn):
    return call(update_kernel, "update", (sums, ws, wn), 3, [shape(ws.shape, F32)] * 2, (0, 1), limit=16)


def exchange(x):
    return lax.all_to_all(x, "dom", split_axis=0, concat_axis=0, tiled=True)


def body(
    feats, edge_src, edge_slot, slot_counts, replica_row, stale_agg, bin_ages, cotangent, w_self, w_neigh
):
    verts, width = feats.shape
    peers, cap = replica_row.shape[1:]
    arrived = exchange(scatter(slot_counts, replica_row, edge_src, edge_slot, feats))
    adj = adjacency(edge_src, edge_slot, verts, peers * cap)
    hidden, grad_pre, aggregate, parts = masters(
        cap, arrived, adj, bin_ages, feats, stale_agg, cotangent, w_self, w_neigh
    )
    parts = exchange(parts)
    sent = outgoing(cap, arrived, grad_pre, aggregate, w_neigh)
    own = summed(parts, sent)
    groups = range(lax.axis_size("group"))
    others = [lax.ppermute(own, "group", [(k, k ^ other) for k in groups]) for other in (1, 2, 3)]
    returned = exchange(sent)
    sums = exchange(tied(shares((own, *others), peers), returned))
    feat_grad = back(cap, returned, grad_pre, slot_counts, adj, w_self)
    new_self, new_neigh = update(sums, w_self, w_neigh)
    return (hidden, feat_grad, new_self, new_neigh)


def solution(mesh):
    both = ("group", "dom")
    wide = P(both, None)
    placed = (wide, wide, wide, wide, P(both, None, None), wide, P(both), wide, P(), P())
    return jax.shard_map(
        body,
        mesh=mesh,
        in_specs=placed,
        out_specs=(wide, wide, P(), P()),
        check_vma=False,
    )
```
